32 devices in a mesh: row: 4 (over y, x), col: 8 (over z, core).
Axes of the slice: x: 2, y: 2, z: 4, core: 2. Of those that a mesh axis runs over, the one named last changes fastest.
Arguments:
- features: float32 [8192, 512], P(('col', 'row')), may hold values from -6 to 6
- weight: float32 [512, 512], replicated, may hold values from -0.25 to 0.25
- tile_values: bfloat16 [4, 8, 32, 256, 256], P('row', 'col'), as said below
- tile_ids: int32 [4, 8, 32, 2], P('row', 'col'), may hold values from 0 to 7, as said below
- tile_counts: int32 [4, 8], P('row', 'col'), may hold values from 1 to 32, as said below
Outputs:
- activated: float32 [8192, 512], P(('row', 'col'))
The draws below stay inside these ranges and needn't reach their ends.
Inputs may be any that keep to these rules, and one draw needn't show every extreme that they name: `tile_counts`: slots at or beyond a panel's count are ignored; some panel holds 32 live slots. `tile_ids`: the first entry is below 8, the second below 4; a tile may repeat. `tile_values`: nonnegative.
All inputs are finite; a program needn't handle non-finite values.
Results may differ from the reference program's by a relative error of at most 0.0003.
Values may be sent and summed in bfloat16 or wider, within the bound.
A program may use at most 128 MiB of HBM per device.

```python
import jax
import jax.numpy as jnp
from jax import lax

TILE_EDGE = 256
F = 512
DEVICE_TILES = 32
N = 8192
RPB = 8
COLUMNS_PER_PANEL = 4
N_ROW = 4
N_COL = 8


def draw_tile_counts(key, part):
    key_first, key_second, key_chosen = jax.random.split(key, 3)
    first_draw = jax.random.randint(key_first, (N_ROW * N_COL,), 1, DEVICE_TILES + 1)
    second_draw = jax.random.randint(key_second, (N_ROW * N_COL,), 1, DEVICE_TILES + 1)
    smaller = jnp.minimum(first_draw, second_draw)
    chosen = jax.random.randint(key_chosen, (), 0, N_ROW * N_COL)
    smaller = smaller.at[chosen].set(DEVICE_TILES)
    return smaller.reshape(N_ROW, N_COL).astype(jnp.int32)


def draw_tile_ids(key, part):
    key_rows, key_columns = jax.random.split(jax.random.fold_in(key, 11), 2)
    row_part = jax.random.randint(key_rows, (N_ROW, N_COL, DEVICE_TILES), 0, RPB)
    column_portion = jax.random.randint(key_columns, (N_ROW, N_COL, DEVICE_TILES), 0, COLUMNS_PER_PANEL)
    return jnp.stack([row_part, column_portion], axis=-1).astype(jnp.int32)


def draw_tile_values(key, part):
    key_base, key_rows, key_columns = jax.random.split(jax.random.fold_in(key, 23), 3)
    base = jax.random.uniform(key_base, (N_ROW, N_COL, DEVICE_TILES, TILE_EDGE, TILE_EDGE), jnp.float32)
    row_scale = jnp.exp(jax.random.uniform(key_rows, (N_ROW, N_COL, DEVICE_TILES, TILE_EDGE, 1), jnp.float32) * 2.302585) * 0.1
    col_scale = jnp.exp(jax.random.uniform(key_columns, (N_ROW, N_COL, DEVICE_TILES, 1, TILE_EDGE), jnp.float32) * 2.302585) * 0.1
    ramp = 1.0 + 2.0 * jnp.arange(N_COL, dtype=jnp.float32) / max(N_COL - 1, 1)
    values = base * row_scale * col_scale * ramp[None, :, None, None, None]
    return values.astype(jnp.bfloat16)


def steps_of(stream_key, shape, cuts, least, high):
    def one(position, shards_of):
        heights = jax.random.uniform(jax.random.fold_in(jax.random.fold_in(stream_key, 6), position), (shards_of,), jnp.float32, least / len(cuts), high / len(cuts))
        return jnp.repeat(jnp.exp(heights), shape[position] // shards_of).reshape((-1,) + (1,) * (len(shape) - position - 1))

    factor_of = one(*cuts[0])
    for cut in cuts[1:]:
        factor_of = factor_of * one(*cut)
    return factor_of


def scatter_about(stream_key, extent, width, reach, cuts=(), kind=jnp.bfloat16):
    gain = steps_of(stream_key, extent, cuts, -0.22, 0.18) if cuts else 1.0
    values = jax.random.normal(stream_key, extent, jnp.float32) * width * gain
    return jnp.minimum(jnp.maximum(values, -reach), reach).astype(kind)


def setup_inputs(seed: int = 0) -> dict:
    key_of = jax.random.split(jax.random.key(seed), 6)
    features = scatter_about(key_of[0], (N, F), 1.0, 6.0, ((0, 32),), jnp.float32)
    weight = scatter_about(key_of[1], (F, F), F ** -0.5, 0.25, (), jnp.float32)
    tile_values = draw_tile_values(jax.random.fold_in(key_of[5], 71), 0)
    tile_ids = draw_tile_ids(jax.random.fold_in(key_of[5], 71), 0)
    tile_counts = draw_tile_counts(jax.random.fold_in(key_of[5], 71), 0)
    return {"features": features, "weight": weight, "tile_values": tile_values, "tile_ids": tile_ids, "tile_counts": tile_counts}


def reference(features, weight, tile_values, tile_ids, tile_counts):
    flat_values = tile_values.reshape(N_ROW * N_COL * DEVICE_TILES, TILE_EDGE, TILE_EDGE)
    flattened_ids = tile_ids.reshape(N_ROW * N_COL * DEVICE_TILES, 2)
    panel_counts = tile_counts.reshape(N_ROW * N_COL)

    def visit_slot(flattened_index, running):
        device = flattened_index // DEVICE_TILES
        slot_index = flattened_index % DEVICE_TILES
        grid_row = device // N_COL
        column_in_grid = device % N_COL

        def apply_tile(state_pair):
            summed, degree = state_pair
            tile_block = flat_values[flattened_index].astype(jnp.float32)
            row_start = ((grid_row * RPB + flattened_ids[flattened_index, 0]) * TILE_EDGE).astype(jnp.int32)
            column_begin = ((column_in_grid * COLUMNS_PER_PANEL + flattened_ids[flattened_index, 1]) * TILE_EDGE).astype(jnp.int32)
            source_rows = lax.dynamic_slice_in_dim(features, column_begin, TILE_EDGE, 0)
            product = jnp.dot(tile_block, source_rows, precision=lax.Precision.HIGHEST)
            old_rows = lax.dynamic_slice_in_dim(summed, row_start, TILE_EDGE, 0)
            summed = lax.dynamic_update_slice_in_dim(summed, old_rows + product, row_start, 0)
            old_degree = lax.dynamic_slice_in_dim(degree, row_start, TILE_EDGE, 0)
            degree = lax.dynamic_update_slice_in_dim(degree, old_degree + lax.optimization_barrier(jnp.sum(tile_block, axis=1)), row_start, 0)
            return (summed, degree)

        def unchanged(state_pair):
            return state_pair
        return lax.cond(slot_index < panel_counts[device], apply_tile, unchanged, running)
    start_pair = (features.astype(jnp.float32), jnp.ones((N,), jnp.float32))
    summed, degree = lax.fori_loop(0, N_ROW * N_COL * DEVICE_TILES, visit_slot, start_pair)
    projected = jnp.dot(summed, weight, precision=lax.Precision.HIGHEST)
    return jnp.maximum(projected * lax.rsqrt(degree)[:, None], 0.0)
```

```python
import functools

import jax
import jax.numpy as jnp
from jax import lax
from jax.experimental import pallas as pl
from jax.experimental.pallas import tpu as pltpu
from jax.sharding import PartitionSpec as P

LANES = 128
CORES = 2
GROUP = 8
QMAX = 32767.0
MESH = pl.DeviceIdType.MESH


def quantize(x, peak):
    inverse = QMAX / peak
    return jnp.round(x * inverse).astype(jnp.int32).astype(jnp.int16)


def row_peak(x):
    return jnp.maximum(jnp.max(jnp.abs(x), axis=1, keepdims=True), 1e-30)


def to_row(column):
    wide = jnp.broadcast_to(column, (LANES, LANES))
    eye = lax.broadcasted_iota(jnp.int32, (LANES, LANES), 0) == lax.broadcasted_iota(
        jnp.int32, (LANES, LANES), 1
    )
    return jnp.sum(jnp.where(eye, wide, 0.0), axis=0, keepdims=True)


def to_columns(row):
    return jnp.broadcast_to(row, (LANES, LANES)).T


def kernel(
    n_row, n_col, chunks, slots,
    feat_hbm, w_hbm, tiles_hbm, ids, count,
    out_ref,
    feat, weight, tiles, w_hi, w_lo,
    gq, gs, gscale, rhs, sums, degs,
    xs, xr, zq, zs, zr, zrs, own, ds, dr,
    last, prevs,
    in_sem, g_send, g_recv, gs_send, gs_recv, x_send, x_recv,
    z_send, z_recv, zs_send, zs_recv, d_send, d_recv,
):
    r = lax.axis_index("row")
    c = lax.axis_index("col")
    n_z = n_col // CORES
    z = c // CORES
    core = c % CORES
    other = 1 - core
    rows = feat.shape[0]
    halves = rows // LANES

    barrier = pltpu.get_barrier_semaphore()

    def greet_row(d, _):
        pl.semaphore_signal(barrier, inc=1, device_id=((r + d) % n_row, c), device_id_type=MESH)
        return 0

    def greet_col(d, _):
        pl.semaphore_signal(barrier, inc=1, device_id=(r, (c + d) % n_col), device_id_type=MESH)
        return 0

    lax.fori_loop(1, n_row, greet_row, 0)
    lax.fori_loop(1, n_col, greet_col, 0)

    load_f = pltpu.make_async_copy(feat_hbm, feat, in_sem.at[0])
    load_t = pltpu.make_async_copy(tiles_hbm, tiles, in_sem.at[1])
    load_w = pltpu.make_async_copy(w_hbm, weight, in_sem.at[2])
    load_f.start()
    load_t.start()
    load_w.start()

    for i in range(n_col):
        last[i] = 0

    def link(s, _):
        row = ids[s, 0]
        live = s < count[0, 0]
        prevs[s] = last[row]
        for i in range(n_col):
            last[i] = jnp.where(live & (row == i), s + 1, last[i])
        return 0

    load_f.wait()
    values = feat[...]
    peak = row_peak(values)
    for h in range(halves):
        gs[r, h : h + 1, :] = to_row(peak[h * LANES : (h + 1) * LANES] * (1.0 / QMAX))
    for k in range(chunks):
        gq[r, k] = quantize(values[:, k * LANES : (k + 1) * LANES], peak)

    pl.semaphore_wait(barrier, n_row + n_col - 2)

    def scale_copy(d, source):
        return pltpu.make_async_remote_copy(
            src_ref=gs.at[source], dst_ref=gs.at[source],
            send_sem=gs_send.at[d], recv_sem=gs_recv.at[d],
            device_id=((r + d) % n_row, c), device_id_type=MESH,
        )

    def gather_copy(k, d, source):
        return pltpu.make_async_remote_copy(
            src_ref=gq.at[source, k], dst_ref=gq.at[source, k],
            send_sem=g_send.at[k, d], recv_sem=g_recv.at[k, d],
            device_id=((r + d) % n_row, c), device_id_type=MESH,
        )

    def send_scale(d, _):
        scale_copy(d, r).start()
        return 0

    lax.fori_loop(1, n_row, send_scale, 0)

    def send_gather(t, _):
        gather_copy(t // (n_row - 1), t % (n_row - 1) + 1, r).start()
        return 0

    lax.fori_loop(0, chunks * (n_row - 1), send_gather, 0)

    lax.fori_loop(0, slots, link, 0)

    load_t.wait()
    degs[0] = jnp.zeros(degs.shape[1:], jnp.float32)
    sums[0] = jnp.zeros(sums.shape[1:], jnp.float32)

    def degree_slot(s, _):
        tile = tiles[s].astype(jnp.float32)
        part = degs[prevs[s]]
        for lane in range(0, tile.shape[1], LANES):
            part = part + tile[:, lane : lane + LANES]
        degs[s + 1] = part
        return 0

    lax.fori_loop(0, slots, degree_slot, 0)

    def degree_block(i, _):
        total = jnp.sum(degs[last[i]], axis=1, keepdims=True)
        for h in range(halves):
            ds[i, h : h + 1, :] = to_row(total[h * LANES : (h + 1) * LANES])
        return 0

    lax.fori_loop(0, n_col, degree_block, 0)

    def degree_copy(d):
        return pltpu.make_async_remote_copy(
            src_ref=ds.at[(c + d) % n_col], dst_ref=dr.at[d],
            send_sem=d_send.at[d], recv_sem=d_recv.at[d],
            device_id=(r, (c + d) % n_col), device_id_type=MESH,
        )

    def send_degree(d, _):
        degree_copy(d).start()
        return 0

    lax.fori_loop(1, n_col, send_degree, 0)

    load_w.wait()
    for k in range(chunks):
        part = weight[k * LANES : (k + 1) * LANES, :]
        high = part.astype(jnp.bfloat16)
        w_hi[k] = high
        w_lo[k] = (part - high.astype(jnp.float32)).astype(jnp.bfloat16)

    def wait_scale(d, _):
        scale_copy(d, (r + n_row - d) % n_row).wait_recv()
        return 0

    lax.fori_loop(1, n_row, wait_scale, 0)

    def spread_scale(j, _):
        for h in range(halves):
            gscale[j, h * LANES : (h + 1) * LANES, :] = to_columns(gs[j, h : h + 1, :])
        return 0

    lax.fori_loop(0, n_row, spread_scale, 0)

    def core_copy(k):
        return pltpu.make_async_remote_copy(
            src_ref=xs.at[k], dst_ref=xr.at[k],
            send_sem=x_send.at[k], recv_sem=x_recv.at[k],
            device_id=(r, z * CORES + other), device_id_type=MESH,
        )

    def z_copy(k, d):
        return pltpu.make_async_remote_copy(
            src_ref=zq.at[k, d], dst_ref=zr.at[k, d],
            send_sem=z_send.at[k, d], recv_sem=z_recv.at[k, d],
            device_id=(r, ((z + d) % n_z) * CORES + core), device_id_type=MESH,
        )

    def zs_copy(k, d):
        return pltpu.make_async_remote_copy(
            src_ref=zs.at[k, d], dst_ref=zrs.at[k, d],
            send_sem=zs_send.at[k, d], recv_sem=zs_recv.at[k, d],
            device_id=(r, ((z + d) % n_z) * CORES + core), device_id_type=MESH,
        )

    def local_block(i):
        j = r * n_col + i - c * n_row
        mine = (j >= 0) & (j < n_row)
        block = rhs[jnp.clip(j, 0, n_row - 1)].astype(jnp.float32)
        block = block[:, :LANES] + block[:, LANES:]
        return sums[last[i]] + jnp.where(mine, block, 0.0)

    def one_chunk(k, _):
        def wait_gather(d, _):
            gather_copy(k, d, (r + n_row - d) % n_row).wait_recv()
            return 0

        lax.fori_loop(1, n_row, wait_gather, 0)

        def decode(j, _):
            value = gq[j, k].astype(jnp.int32).astype(jnp.float32) * gscale[j]
            high = value.astype(jnp.bfloat16)
            rhs[j, :, :LANES] = high
            rhs[j, :, LANES:] = (value - high.astype(jnp.float32)).astype(jnp.bfloat16)
            return 0

        lax.fori_loop(0, n_row, decode, 0)

        def products(g, _):
            found = []
            for u in range(GROUP):
                s = g * GROUP + u
                both = jnp.dot(tiles[s], rhs[ids[s, 1]], preferred_element_type=jnp.float32)
                found.append(both[:, :LANES] + both[:, LANES:])
            for u in range(GROUP):
                s = g * GROUP + u
                sums[s + 1] = found[u] + sums[prevs[s]]
            return 0

        lax.fori_loop(0, slots // GROUP, products, 0)

        def hand_over(zz, _):
            xs[k, zz] = local_block(zz * CORES + other)
            return 0

        lax.fori_loop(0, n_z, hand_over, 0)
        core_copy(k).start()
        core_copy(k).wait_recv()

        def send_z(d, _):
            zz = (z + d) % n_z
            value = local_block(zz * CORES + core) + xr[k, zz]
            peak = row_peak(value)
            for h in range(halves):
                zs[k, d, h : h + 1, :] = to_row(peak[h * LANES : (h + 1) * LANES] * (1.0 / QMAX))
            zq[k, d] = quantize(value, peak)
            zs_copy(k, d).start()
            z_copy(k, d).start()
            return 0

        lax.fori_loop(1, n_z, send_z, 0)
        own[k] = local_block(z * CORES + core) + xr[k, z]
        return 0

    lax.fori_loop(0, chunks, one_chunk, 0)

    def add_degree(d, total):
        degree_copy(d).wait_recv()
        return total + dr[d]

    degree = lax.fori_loop(1, n_col, add_degree, 1.0 + ds[c])
    root = lax.rsqrt(degree)

    out_ref[...] = jnp.zeros(out_ref.shape, jnp.float32)

    def finish(k, _):
        def add_z(d, _):
            zs_copy(k, d).wait_recv()
            z_copy(k, d).wait_recv()
            for h in range(halves):
                part = slice(h * LANES, (h + 1) * LANES)
                scale = to_columns(zrs[k, d, h : h + 1, :])
                own[k, part] += zr[k, d, part].astype(jnp.int32).astype(jnp.float32) * scale
            return 0

        lax.fori_loop(1, n_z, add_z, 0)
        total = own[k]
        high = total.astype(jnp.bfloat16)
        low = (total - high.astype(jnp.float32)).astype(jnp.bfloat16)
        dot = functools.partial(jnp.dot, preferred_element_type=jnp.float32)
        out_ref[...] += dot(high, w_hi[k]) + (dot(high, w_lo[k]) + dot(low, w_hi[k]))
        return 0

    lax.fori_loop(0, chunks, finish, 0)
    for h in range(halves):
        part = slice(h * LANES, (h + 1) * LANES)
        factor = to_columns(root[h : h + 1, :])
        for k in range(chunks):
            cols = slice(k * LANES, (k + 1) * LANES)
            out_ref[part, cols] = jnp.maximum(out_ref[part, cols] * factor, 0.0)

    def drain_row(d, _):
        scale_copy(d, r).wait_send()

        def drain_chunk(k, _):
            gather_copy(k, d, r).wait_send()
            return 0

        lax.fori_loop(0, chunks, drain_chunk, 0)
        return 0

    def drain_degree(d, _):
        degree_copy(d).wait_send()
        return 0

    def drain_core(k, _):
        core_copy(k).wait_send()

        def drain_z(d, _):
            z_copy(k, d).wait_send()
            zs_copy(k, d).wait_send()
            return 0

        lax.fori_loop(1, n_z, drain_z, 0)
        return 0

    lax.fori_loop(1, n_row, drain_row, 0)
    lax.fori_loop(1, n_col, drain_degree, 0)
    lax.fori_loop(0, chunks, drain_core, 0)


def solution(mesh):
    n_row, n_col = mesh.shape["row"], mesh.shape["col"]
    n_z = n_col // CORES

    def shards(features, weight, tile_values, tile_ids, tile_counts):
        rows, width = features.shape
        slots, edge = tile_values.shape[2], tile_values.shape[3]
        chunks = width // LANES
        halves = rows // LANES
        f32, bf16, i16 = jnp.float32, jnp.bfloat16, jnp.int16
        dma = pltpu.SemaphoreType.DMA
        hbm = pl.BlockSpec(memory_space=pl.ANY)
        smem = pl.BlockSpec(memory_space=pltpu.SMEM)
        vmem = pl.BlockSpec(memory_space=pltpu.VMEM)
        return pl.pallas_call(
            functools.partial(kernel, n_row, n_col, chunks, slots),
            out_shape=jax.ShapeDtypeStruct((rows, width), f32),
            in_specs=[hbm, hbm, hbm, smem, smem],
            out_specs=vmem,
            scratch_shapes=[
                pltpu.VMEM((rows, width), f32),
                pltpu.VMEM((width, width), f32),
                pltpu.VMEM((slots, edge, edge), bf16),
                pltpu.VMEM((chunks, LANES, width), bf16),
                pltpu.VMEM((chunks, LANES, width), bf16),
                pltpu.VMEM((n_row, chunks, rows, LANES), i16),
                pltpu.VMEM((n_row, halves, LANES), f32),
                pltpu.VMEM((n_row, rows, LANES), f32),
                pltpu.VMEM((n_row, rows, 2 * LANES), bf16),
                pltpu.VMEM((slots + 1, edge, LANES), f32),
                pltpu.VMEM((slots + 1, edge, LANES), f32),
                pltpu.VMEM((chunks, n_z, rows, LANES), f32),
                pltpu.VMEM((chunks, n_z, rows, LANES), f32),
                pltpu.VMEM((chunks, n_z, rows, LANES), i16),
                pltpu.VMEM((chunks, n_z, halves, LANES), f32),
                pltpu.VMEM((chunks, n_z, rows, LANES), i16),
                pltpu.VMEM((chunks, n_z, halves, LANES), f32),
                pltpu.VMEM((chunks, rows, LANES), f32),
                pltpu.VMEM((n_col, halves, LANES), f32),
                pltpu.VMEM((n_col, halves, LANES), f32),
                pltpu.SMEM((n_col,), jnp.int32),
                pltpu.SMEM((slots,), jnp.int32),
                dma((3,)),
                dma((chunks, n_row)),
                dma((chunks, n_row)),
                dma((n_row,)),
                dma((n_row,)),
                dma((chunks,)),
                dma((chunks,)),
                dma((chunks, n_z)),
                dma((chunks, n_z)),
                dma((chunks, n_z)),
                dma((chunks, n_z)),
                dma((n_col,)),
                dma((n_col,)),
            ],
            compiler_params=pltpu.CompilerParams(
                collective_id=0, has_side_effects=True, vmem_limit_bytes=56 * 1024 * 1024
            ),
        )(
            features,
            weight,
            tile_values.reshape(slots, edge, edge),
            tile_ids.reshape(slots, 2),
            tile_counts,
        )

    in_specs = (
        P(("col", "row"), None),
        P(),
        P("row", "col", None, None, None),
        P("row", "col", None, None),
        P("row", "col"),
    )
    out_specs = P(("row", "col"), None)
    return jax.shard_map(shards, mesh=mesh, in_specs=in_specs, out_specs=out_specs, check_vma=False)
```

```python
import functools

import jax
import jax.numpy as jnp
from jax import lax
from jax.experimental import pallas as pl
from jax.experimental.pallas import tpu as pltpu
from jax.sharding import PartitionSpec as P

LANES = 128
CORES = 2
GROUP = 8
QMAX = 32767.0
MESH = pl.DeviceIdType.MESH


def quantize(x, peak):
    inverse = QMAX / peak
    return jnp.round(x * inverse).astype(jnp.int32).astype(jnp.int16)


def row_peak(x):
    return jnp.maximum(jnp.max(jnp.abs(x), axis=1, keepdims=True), 1e-30)


def to_row(column):
    wide = jnp.broadcast_to(column, (LANES, LANES))
    eye = lax.broadcasted_iota(jnp.int32, (LANES, LANES), 0) == lax.broadcasted_iota(
        jnp.int32, (LANES, LANES), 1
    )
    return jnp.sum(jnp.where(eye, wide, 0.0), axis=0, keepdims=True)


def to_columns(row):
    return jnp.broadcast_to(row, (LANES, LANES)).T


def kernel(
    n_row, n_col, chunks, slots,
    feat_hbm, w_hbm, tiles_hbm, ids, count,
    out_ref,
    feat, weight, tiles, w_hi, w_lo,
    gq, gs, gscale, rhs, sums, degs,
    xs, xr, zq, zs, zr, zrs, ds, dr,
    last, prevs,
    in_sem, g_send, g_recv, gs_send, gs_recv, x_send, x_recv,
    z_send, z_recv, zs_send, zs_recv, d_send, d_recv,
):
    r = lax.axis_index("row")
    c = lax.axis_index("col")
    n_z = n_col // CORES
    z = c // CORES
    core = c % CORES
    other = 1 - core
    rows = feat.shape[0]
    halves = rows // LANES

    barrier = pltpu.get_barrier_semaphore()

    def greet_row(d, _):
        pl.semaphore_signal(barrier, inc=1, device_id=((r + d) % n_row, c), device_id_type=MESH)
        return 0

    def greet_col(d, _):
        pl.semaphore_signal(barrier, inc=1, device_id=(r, (c + d) % n_col), device_id_type=MESH)
        return 0

    lax.fori_loop(1, n_row, greet_row, 0)
    lax.fori_loop(1, n_col, greet_col, 0)

    load_f = pltpu.make_async_copy(feat_hbm, feat, in_sem.at[0])
    load_t = pltpu.make_async_copy(tiles_hbm, tiles, in_sem.at[1])
    load_w = pltpu.make_async_copy(w_hbm, weight, in_sem.at[2])
    load_f.start()
    load_t.start()
    load_w.start()

    for i in range(n_col):
        last[i] = 0

    def link(s, _):
        row = ids[0, s]
        live = s < count[0, 0]
        prevs[s] = last[row]
        for i in range(n_col):
            last[i] = jnp.where(live & (row == i), s + 1, last[i])
        return 0

    load_f.wait()
    values = feat[...]
    peak = row_peak(values)
    for h in range(halves):
        gs[r, h : h + 1, :] = to_row(peak[h * LANES : (h + 1) * LANES] * (1.0 / QMAX))
    for k in range(chunks):
        gq[r, k] = quantize(values[:, k * LANES : (k + 1) * LANES], peak)

    pl.semaphore_wait(barrier, n_row + n_col - 2)

    def scale_copy(d, source):
        return pltpu.make_async_remote_copy(
            src_ref=gs.at[source], dst_ref=gs.at[source],
            send_sem=gs_send.at[d], recv_sem=gs_recv.at[d],
            device_id=((r + d) % n_row, c), device_id_type=MESH,
        )

    def gather_copy(k, d, source):
        return pltpu.make_async_remote_copy(
            src_ref=gq.at[source, k], dst_ref=gq.at[source, k],
            send_sem=g_send.at[k, d], recv_sem=g_recv.at[k, d],
            device_id=((r + d) % n_row, c), device_id_type=MESH,
        )

    def send_scale(d, _):
        scale_copy(d, r).start()
        return 0

    lax.fori_loop(1, n_row, send_scale, 0)

    def send_gather(k):
        def send(d, _):
            gather_copy(k, d, r).start()
            return 0

        lax.fori_loop(1, n_row, send, 0)

    send_gather(0)

    lax.fori_loop(0, slots, link, 0)

    load_t.wait()
    degs[0] = jnp.zeros(degs.shape[1:], jnp.float32)
    sums[0] = jnp.zeros(sums.shape[1:], jnp.float32)

    def degree_slot(s, _):
        tile = tiles[s].astype(jnp.float32)
        part = degs[prevs[s]]
        for lane in range(0, tile.shape[1], LANES):
            part = part + tile[:, lane : lane + LANES]
        degs[s + 1] = part
        return 0

    lax.fori_loop(0, slots, degree_slot, 0)

    def degree_block(i, _):
        total = jnp.sum(degs[last[i]], axis=1, keepdims=True)
        for h in range(halves):
            ds[i, h : h + 1, :] = to_row(total[h * LANES : (h + 1) * LANES])
        return 0

    lax.fori_loop(0, n_col, degree_block, 0)

    def degree_copy(d):
        return pltpu.make_async_remote_copy(
            src_ref=ds.at[(c + d) % n_col], dst_ref=dr.at[d],
            send_sem=d_send.at[d], recv_sem=d_recv.at[d],
            device_id=(r, (c + d) % n_col), device_id_type=MESH,
        )

    def send_degree(d, _):
        degree_copy(d).start()
        return 0

    lax.fori_loop(1, n_col, send_degree, 0)

    load_w.wait()
    for k in range(chunks):
        part = weight[k * LANES : (k + 1) * LANES, :]
        high = part.astype(jnp.bfloat16)
        w_hi[k] = high
        w_lo[k] = (part - high.astype(jnp.float32)).astype(jnp.bfloat16)

    def wait_scale(d, _):
        scale_copy(d, (r + n_row - d) % n_row).wait_recv()
        return 0

    lax.fori_loop(1, n_row, wait_scale, 0)

    def spread_scale(j, _):
        for h in range(halves):
            gscale[j, h * LANES : (h + 1) * LANES, :] = to_columns(gs[j, h : h + 1, :])
        return 0

    lax.fori_loop(0, n_row, spread_scale, 0)

    def core_copy(k):
        return pltpu.make_async_remote_copy(
            src_ref=xs.at[k], dst_ref=xr.at[k],
            send_sem=x_send.at[k], recv_sem=x_recv.at[k],
            device_id=(r, z * CORES + other), device_id_type=MESH,
        )

    def z_copy(way, k, d):
        step = 1 - 2 * way
        target = jnp.clip(z + step, 0, n_z - 1) * CORES + core
        at = way * chunks + k
        return [
            pltpu.make_async_remote_copy(
                src_ref=source.at[at, d], dst_ref=landing.at[at, d],
                send_sem=sent.at[at, d], recv_sem=landed.at[at, d],
                device_id=(r, target), device_id_type=MESH,
            )
            for source, landing, sent, landed in (
                (zs, zrs, zs_send, zs_recv), (zq, zr, z_send, z_recv),
            )
        ]

    def received(way, k, d):
        for copy in z_copy(way, k, d):
            copy.wait_recv()
        at = way * chunks + k
        parts = []
        for h in range(halves):
            scale = to_columns(zrs[at, d, h : h + 1, :])
            code = zr[at, d, h * LANES : (h + 1) * LANES]
            parts.append(code.astype(jnp.int32).astype(jnp.float32) * scale)
        return jnp.concatenate(parts, axis=0)

    def hand_on(way, k, d, value):
        at = way * chunks + k
        peak = row_peak(value)
        for h in range(halves):
            zs[at, d, h : h + 1, :] = to_row(peak[h * LANES : (h + 1) * LANES] * (1.0 / QMAX))
        zq[at, d] = quantize(value, peak)
        for copy in z_copy(way, k, d):
            copy.start()

    top = n_z - 1

    def begin(k):
        def step(t, _):
            @pl.when((z == 0) & (t < top))
            def _():
                hand_on(0, k, top - t, xr[k, top - t])

            @pl.when((z == top) & (t < top))
            def _():
                hand_on(1, k, t, xr[k, t])

            return 0

        lax.fori_loop(0, top, step, 0)

    def relay(k):
        def step(t, _):
            up = top - (t - z)

            @pl.when((z > 0) & (t >= z) & (up > z))
            def _():
                hand_on(0, k, up, xr[k, up] + received(0, k, up))

            down = t - (top - z)

            @pl.when((z < top) & (down >= 0) & (down < z))
            def _():
                hand_on(1, k, down, xr[k, down] + received(1, k, down))

            return 0

        lax.fori_loop(1, top, step, 0)

    def local_block(i):
        j = r * n_col + i - c * n_row
        mine = (j >= 0) & (j < n_row)
        block = rhs[jnp.clip(j, 0, n_row - 1)].astype(jnp.float32)
        block = block[:, :LANES] + block[:, LANES:]
        return sums[last[i]] + jnp.where(mine, block, 0.0)

    def one_chunk(k, _):
        def wait_gather(d, _):
            gather_copy(k, d, (r + n_row - d) % n_row).wait_recv()
            return 0

        lax.fori_loop(1, n_row, wait_gather, 0)

        @pl.when(k + 1 < chunks)
        def _():
            send_gather(k + 1)

        def decode(j, _):
            value = gq[j, k].astype(jnp.int32).astype(jnp.float32) * gscale[j]
            high = value.astype(jnp.bfloat16)
            rhs[j, :, :LANES] = high
            rhs[j, :, LANES:] = (value - high.astype(jnp.float32)).astype(jnp.bfloat16)
            return 0

        lax.fori_loop(0, n_row, decode, 0)

        def products(g, _):
            found = []
            for u in range(GROUP):
                s = g * GROUP + u
                both = jnp.dot(tiles[s], rhs[ids[1, s]], preferred_element_type=jnp.float32)
                found.append(both[:, :LANES] + both[:, LANES:])
            for u in range(GROUP):
                s = g * GROUP + u
                sums[s + 1] = found[u] + sums[prevs[s]]
            return 0

        lax.fori_loop(0, slots // GROUP, products, 0)

        def hand_over(zz, _):
            xs[k, zz] = local_block(zz * CORES + other)
            return 0

        lax.fori_loop(0, n_z, hand_over, 0)
        core_copy(k).start()
        core_copy(k).wait_recv()

        def add_own(zz, _):
            xr[k, zz] += local_block(zz * CORES + core)
            return 0

        lax.fori_loop(0, n_z, add_own, 0)
        begin(k)

        @pl.when(k > 0)
        def _():
            relay(k - 1)

        return 0

    lax.fori_loop(0, chunks, one_chunk, 0)
    relay(chunks - 1)

    def add_degree(d, total):
        degree_copy(d).wait_recv()
        return total + dr[d]

    degree = lax.fori_loop(1, n_col, add_degree, 1.0 + ds[c])
    root = lax.rsqrt(degree)

    out_ref[...] = jnp.zeros(out_ref.shape, jnp.float32)

    def finish(k, _):
        @pl.when(z > 0)
        def _():
            xr[k, z] += received(0, k, z)

        @pl.when(z < top)
        def _():
            xr[k, z] += received(1, k, z)

        total = xr[k, z]
        high = total.astype(jnp.bfloat16)
        low = (total - high.astype(jnp.float32)).astype(jnp.bfloat16)
        dot = functools.partial(jnp.dot, preferred_element_type=jnp.float32)
        out_ref[...] += dot(high, w_hi[k]) + (dot(high, w_lo[k]) + dot(low, w_hi[k]))
        return 0

    lax.fori_loop(0, chunks, finish, 0)
    for h in range(halves):
        part = slice(h * LANES, (h + 1) * LANES)
        factor = to_columns(root[h : h + 1, :])
        for k in range(chunks):
            cols = slice(k * LANES, (k + 1) * LANES)
            out_ref[part, cols] = jnp.maximum(out_ref[part, cols] * factor, 0.0)

    def drain_row(d, _):
        scale_copy(d, r).wait_send()

        def drain_chunk(k, _):
            gather_copy(k, d, r).wait_send()
            return 0

        lax.fori_loop(0, chunks, drain_chunk, 0)
        return 0

    def drain_degree(d, _):
        degree_copy(d).wait_send()
        return 0

    def drain_core(k, _):
        core_copy(k).wait_send()

        def drain_z(d, _):
            @pl.when(d > z)
            def _():
                for copy in z_copy(0, k, d):
                    copy.wait_send()

            @pl.when(d < z)
            def _():
                for copy in z_copy(1, k, d):
                    copy.wait_send()

            return 0

        lax.fori_loop(0, n_z, drain_z, 0)
        return 0

    lax.fori_loop(1, n_row, drain_row, 0)
    lax.fori_loop(1, n_col, drain_degree, 0)
    lax.fori_loop(0, chunks, drain_core, 0)


def solution(mesh):
    n_row, n_col = mesh.shape["row"], mesh.shape["col"]
    n_z = n_col // CORES

    def shards(features, weight, tile_values, tile_ids, tile_counts):
        rows, width = features.shape
        slots, edge = tile_values.shape[2], tile_values.shape[3]
        chunks = width // LANES
        halves = rows // LANES
        f32, bf16, i16 = jnp.float32, jnp.bfloat16, jnp.int16
        dma = pltpu.SemaphoreType.DMA
        hbm = pl.BlockSpec(memory_space=pl.ANY)
        smem = pl.BlockSpec(memory_space=pltpu.SMEM)
        vmem = pl.BlockSpec(memory_space=pltpu.VMEM)
        return pl.pallas_call(
            functools.partial(kernel, n_row, n_col, chunks, slots),
            out_shape=jax.ShapeDtypeStruct((rows, width), f32),
            in_specs=[hbm, hbm, hbm, smem, smem],
            out_specs=vmem,
            scratch_shapes=[
                pltpu.VMEM((rows, width), f32),
                pltpu.VMEM((width, width), f32),
                pltpu.VMEM((slots, edge, edge), bf16),
                pltpu.VMEM((chunks, LANES, width), bf16),
                pltpu.VMEM((chunks, LANES, width), bf16),
                pltpu.VMEM((n_row, chunks, rows, LANES), i16),
                pltpu.VMEM((n_row, halves, LANES), f32),
                pltpu.VMEM((n_row, rows, LANES), f32),
                pltpu.VMEM((n_row, rows, 2 * LANES), bf16),
                pltpu.VMEM((slots + 1, edge, LANES), f32),
                pltpu.VMEM((slots + 1, edge, LANES), f32),
                pltpu.VMEM((chunks, n_z, rows, LANES), f32),
                pltpu.VMEM((chunks, n_z, rows, LANES), f32),
                pltpu.VMEM((2 * chunks, n_z, rows, LANES), i16),
                pltpu.VMEM((2 * chunks, n_z, halves, LANES), f32),
                pltpu.VMEM((2 * chunks, n_z, rows, LANES), i16),
                pltpu.VMEM((2 * chunks, n_z, halves, LANES), f32),
                pltpu.VMEM((n_col, halves, LANES), f32),
                pltpu.VMEM((n_col, halves, LANES), f32),
                pltpu.SMEM((n_col,), jnp.int32),
                pltpu.SMEM((slots,), jnp.int32),
                dma((3,)),
                dma((chunks, n_row)),
                dma((chunks, n_row)),
                dma((n_row,)),
                dma((n_row,)),
                dma((chunks,)),
                dma((chunks,)),
                dma((2 * chunks, n_z)),
                dma((2 * chunks, n_z)),
                dma((2 * chunks, n_z)),
                dma((2 * chunks, n_z)),
                dma((n_col,)),
                dma((n_col,)),
            ],
            compiler_params=pltpu.CompilerParams(
                collective_id=0, has_side_effects=True, vmem_limit_bytes=56 * 1024 * 1024
            ),
        )(
            features,
            weight,
            tile_values.reshape(slots, edge, edge),
            tile_ids.reshape(slots, 2).T,
            tile_counts,
        )

    in_specs = (
        P(("col", "row"), None),
        P(),
        P("row", "col", None, None, None),
        P("row", "col", None, None),
        P("row", "col"),
    )
    out_specs = P(("row", "col"), None)
    return jax.shard_map(shards, mesh=mesh, in_specs=in_specs, out_specs=out_specs, check_vma=False)
```

```python
import functools

import jax
import jax.numpy as jnp
from jax import lax
from jax.experimental import pallas as pl
from jax.experimental.pallas import tpu as pltpu
from jax.sharding import PartitionSpec as P

LANES = 128
CORES = 2
GROUP = 8
QMAX = 32767.0
MESH = pl.DeviceIdType.MESH


def quantize(x, peak):
    inverse = QMAX / peak
    return jnp.round(x * inverse).astype(jnp.int32).astype(jnp.int16)


def row_peak(x):
    return jnp.maximum(jnp.max(jnp.abs(x), axis=1, keepdims=True), 1e-30)


def to_row(column):
    wide = jnp.broadcast_to(column, (LANES, LANES))
    eye = lax.broadcasted_iota(jnp.int32, (LANES, LANES), 0) == lax.broadcasted_iota(
        jnp.int32, (LANES, LANES), 1
    )
    return jnp.sum(jnp.where(eye, wide, 0.0), axis=0, keepdims=True)


def to_columns(row):
    return jnp.broadcast_to(row, (LANES, LANES)).T


def kernel(
    n_row, n_col, chunks, slots,
    feat_hbm, w_hbm, tiles_hbm, ids, count,
    out_ref,
    feat, weight, tiles, w_hi, w_lo,
    gq, gs, gscale, rhs, sums, degs,
    xs, xr, zq, zs, zr, zrs, own, mine, ds, dr,
    last, prevs,
    in_sem, g_send, g_recv, gs_send, gs_recv, x_send, x_recv,
    z_send, z_recv, zs_send, zs_recv, d_send, d_recv,
):
    r = lax.axis_index("row")
    c = lax.axis_index("col")
    n_z = n_col // CORES
    z = c // CORES
    core = c % CORES
    other = 1 - core
    rows = feat.shape[0]
    halves = rows // LANES

    barrier = pltpu.get_barrier_semaphore()

    def greet_row(d, _):
        pl.semaphore_signal(barrier, inc=1, device_id=((r + d) % n_row, c), device_id_type=MESH)
        return 0

    def greet_col(d, _):
        pl.semaphore_signal(barrier, inc=1, device_id=(r, (c + d) % n_col), device_id_type=MESH)
        return 0

    lax.fori_loop(1, n_row, greet_row, 0)
    lax.fori_loop(1, n_col, greet_col, 0)

    load_f = pltpu.make_async_copy(feat_hbm, feat, in_sem.at[0])
    load_t = pltpu.make_async_copy(tiles_hbm, tiles, in_sem.at[1])
    load_w = pltpu.make_async_copy(w_hbm, weight, in_sem.at[2])
    load_f.start()
    load_t.start()
    load_w.start()

    for i in range(n_col):
        last[i] = 0

    def link(s, _):
        row = ids[0, s]
        live = s < count[0, 0]
        prevs[s] = last[row]
        for i in range(n_col):
            last[i] = jnp.where(live & (row == i), s + 1, last[i])
        return 0

    load_f.wait()
    values = feat[...]
    peak = row_peak(values)
    for h in range(halves):
        gs[r, h : h + 1, :] = to_row(peak[h * LANES : (h + 1) * LANES] * (1.0 / QMAX))
    for k in range(chunks):
        gq[r, k] = quantize(values[:, k * LANES : (k + 1) * LANES], peak)

    pl.semaphore_wait(barrier, n_row + n_col - 2)

    def scale_copy(d, source):
        return pltpu.make_async_remote_copy(
            src_ref=gs.at[source], dst_ref=gs.at[source],
            send_sem=gs_send.at[d], recv_sem=gs_recv.at[d],
            device_id=((r + d) % n_row, c), device_id_type=MESH,
        )

    def gather_copy(k, d, source):
        return pltpu.make_async_remote_copy(
            src_ref=gq.at[source, k], dst_ref=gq.at[source, k],
            send_sem=g_send.at[k, d], recv_sem=g_recv.at[k, d],
            device_id=((r + d) % n_row, c), device_id_type=MESH,
        )

    def send_scale(d, _):
        scale_copy(d, r).start()
        return 0

    lax.fori_loop(1, n_row, send_scale, 0)

    def send_gather(k):
        def send(d, _):
            gather_copy(k, d, r).start()
            return 0

        lax.fori_loop(1, n_row, send, 0)

    send_gather(0)

    lax.fori_loop(0, slots, link, 0)

    load_t.wait()
    sums[0] = jnp.zeros(sums.shape[1:], jnp.float32)

    def degree_copy(d):
        return pltpu.make_async_remote_copy(
            src_ref=ds.at[(c + d) % n_col], dst_ref=dr.at[d],
            send_sem=d_send.at[d], recv_sem=d_recv.at[d],
            device_id=(r, (c + d) % n_col), device_id_type=MESH,
        )

    def core_copy(k, d):
        return pltpu.make_async_remote_copy(
            src_ref=xs.at[k, d], dst_ref=xr.at[k, d],
            send_sem=x_send.at[k, d], recv_sem=x_recv.at[k, d],
            device_id=(r, z * CORES + other), device_id_type=MESH,
        )

    def z_copy(k, d):
        return pltpu.make_async_remote_copy(
            src_ref=zq.at[k, d], dst_ref=zr.at[k, d],
            send_sem=z_send.at[k, d], recv_sem=z_recv.at[k, d],
            device_id=(r, ((z + d) % n_z) * CORES + core), device_id_type=MESH,
        )

    def zs_copy(k, d):
        return pltpu.make_async_remote_copy(
            src_ref=zs.at[k, d], dst_ref=zrs.at[k, d],
            send_sem=zs_send.at[k, d], recv_sem=zs_recv.at[k, d],
            device_id=(r, ((z + d) % n_z) * CORES + core), device_id_type=MESH,
        )

    def local_block(i):
        j = r * n_col + i - c * n_row
        inside = (j >= 0) & (j < n_row)
        block = rhs[jnp.clip(j, 0, n_row - 1)].astype(jnp.float32)
        block = block[:, :LANES] + block[:, LANES:]
        return sums[last[i]] + jnp.where(inside, block, 0.0)

    def row_sums():
        degs[0] = jnp.zeros(degs.shape[1:], jnp.float32)

        def degree_slot(s, _):
            tile = tiles[s].astype(jnp.float32)
            part = degs[prevs[s]]
            for lane in range(0, tile.shape[1], LANES):
                part = part + tile[:, lane : lane + LANES]
            degs[s + 1] = part
            return 0

        lax.fori_loop(0, slots, degree_slot, 0)

        def degree_block(i, _):
            total = jnp.sum(degs[last[i]], axis=1, keepdims=True)
            for h in range(halves):
                ds[i, h : h + 1, :] = to_row(total[h * LANES : (h + 1) * LANES])
            return 0

        lax.fori_loop(0, n_col, degree_block, 0)

        def send_degree(d, _):
            degree_copy(d).start()
            return 0

        lax.fori_loop(1, n_col, send_degree, 0)

    def split_weight():
        load_w.wait()
        for k in range(chunks):
            part = weight[k * LANES : (k + 1) * LANES, :]
            high = part.astype(jnp.bfloat16)
            w_hi[k] = high
            w_lo[k] = (part - high.astype(jnp.float32)).astype(jnp.bfloat16)

    def received(k, d):
        zs_copy(k, d).wait_recv()
        z_copy(k, d).wait_recv()
        parts = []
        for h in range(halves):
            code = zr[k, d, h * LANES : (h + 1) * LANES]
            scale = to_columns(zrs[k, d, h : h + 1, :])
            parts.append(code.astype(jnp.int32).astype(jnp.float32) * scale)
        return jnp.concatenate(parts, axis=0)

    def project(k):
        def add_z(d, _):
            own[k] += received(k, d)
            return 0

        lax.fori_loop(1, n_z, add_z, 0)
        total = own[k]
        high = total.astype(jnp.bfloat16)
        low = (total - high.astype(jnp.float32)).astype(jnp.bfloat16)
        dot = functools.partial(jnp.dot, preferred_element_type=jnp.float32)
        out_ref[...] += dot(high, w_hi[k]) + (dot(high, w_lo[k]) + dot(low, w_hi[k]))

    def one_chunk(k, _):
        def wait_gather(d, _):
            gather_copy(k, d, (r + n_row - d) % n_row).wait_recv()
            return 0

        lax.fori_loop(1, n_row, wait_gather, 0)

        @pl.when(k + 1 < chunks)
        def _():
            send_gather(k + 1)

        def decode(j, _):
            value = gq[j, k].astype(jnp.int32).astype(jnp.float32) * gscale[j]
            high = value.astype(jnp.bfloat16)
            rhs[j, :, :LANES] = high
            rhs[j, :, LANES:] = (value - high.astype(jnp.float32)).astype(jnp.bfloat16)
            return 0

        lax.fori_loop(0, n_row, decode, 0)

        def products(g, _):
            for u in range(GROUP):
                s = g * GROUP + u
                both = jnp.dot(tiles[s], rhs[ids[1, s]], preferred_element_type=jnp.float32)
                sums[s + 1] = both[:, :LANES] + both[:, LANES:] + sums[prevs[s]]
            return 0

        lax.fori_loop(0, slots // GROUP, products, 0)

        def hand_over(d, _):
            zz = (z + d) % n_z
            xs[k, d] = local_block(zz * CORES + other)
            core_copy(k, d).start()
            return 0

        lax.fori_loop(1, n_z + 1, hand_over, 0)

        def keep(d, _):
            mine[d] = local_block((z + d) % n_z * CORES + core)
            return 0

        lax.fori_loop(1, n_z + 1, keep, 0)

        @pl.when(k == 0)
        def _():
            split_weight()

        @pl.when(k >= 2)
        def _():
            project(k - 2)

        def send_z(d, _):
            core_copy(k, d).wait_recv()
            value = mine[d] + xr[k, d]
            peak = row_peak(value)
            for h in range(halves):
                zs[k, d, h : h + 1, :] = to_row(peak[h * LANES : (h + 1) * LANES] * (1.0 / QMAX))
            zq[k, d] = quantize(value, peak)
            zs_copy(k, d).start()
            z_copy(k, d).start()
            return 0

        lax.fori_loop(1, n_z, send_z, 0)
        core_copy(k, n_z).wait_recv()
        own[k] = mine[n_z] + xr[k, n_z]
        return 0

    row_sums()

    def wait_scale(d, _):
        scale_copy(d, (r + n_row - d) % n_row).wait_recv()
        return 0

    lax.fori_loop(1, n_row, wait_scale, 0)

    def spread_scale(j, _):
        for h in range(halves):
            gscale[j, h * LANES : (h + 1) * LANES, :] = to_columns(gs[j, h : h + 1, :])
        return 0

    lax.fori_loop(0, n_row, spread_scale, 0)
    out_ref[...] = jnp.zeros(out_ref.shape, jnp.float32)
    lax.fori_loop(0, chunks, one_chunk, 0)

    def add_degree(d, total):
        degree_copy(d).wait_recv()
        return total + dr[d]

    degree = lax.fori_loop(1, n_col, add_degree, 1.0 + ds[c])
    root = lax.rsqrt(degree)

    for k in range(max(chunks - 2, 0), chunks):
        project(k)
    for h in range(halves):
        part = slice(h * LANES, (h + 1) * LANES)
        factor = to_columns(root[h : h + 1, :])
        for k in range(chunks):
            cols = slice(k * LANES, (k + 1) * LANES)
            out_ref[part, cols] = jnp.maximum(out_ref[part, cols] * factor, 0.0)

    def drain_row(d, _):
        scale_copy(d, r).wait_send()

        def drain_chunk(k, _):
            gather_copy(k, d, r).wait_send()
            return 0

        lax.fori_loop(0, chunks, drain_chunk, 0)
        return 0

    def drain_degree(d, _):
        degree_copy(d).wait_send()
        return 0

    def drain_core(k, _):
        def drain_x(d, _):
            core_copy(k, d).wait_send()
            return 0

        lax.fori_loop(1, n_z + 1, drain_x, 0)

        def drain_z(d, _):
            z_copy(k, d).wait_send()
            zs_copy(k, d).wait_send()
            return 0

        lax.fori_loop(1, n_z, drain_z, 0)
        return 0

    lax.fori_loop(1, n_row, drain_row, 0)
    lax.fori_loop(1, n_col, drain_degree, 0)
    lax.fori_loop(0, chunks, drain_core, 0)


def solution(mesh):
    n_row, n_col = mesh.shape["row"], mesh.shape["col"]
    n_z = n_col // CORES

    def shards(features, weight, tile_values, tile_ids, tile_counts):
        rows, width = features.shape
        slots, edge = tile_values.shape[2], tile_values.shape[3]
        chunks = width // LANES
        halves = rows // LANES
        f32, bf16, i16 = jnp.float32, jnp.bfloat16, jnp.int16
        dma = pltpu.SemaphoreType.DMA
        hbm = pl.BlockSpec(memory_space=pl.ANY)
        smem = pl.BlockSpec(memory_space=pltpu.SMEM)
        vmem = pl.BlockSpec(memory_space=pltpu.VMEM)
        return pl.pallas_call(
            functools.partial(kernel, n_row, n_col, chunks, slots),
            out_shape=jax.ShapeDtypeStruct((rows, width), f32),
            in_specs=[hbm, hbm, hbm, smem, smem],
            out_specs=vmem,
            scratch_shapes=[
                pltpu.VMEM((rows, width), f32),
                pltpu.VMEM((width, width), f32),
                pltpu.VMEM((slots, edge, edge), bf16),
                pltpu.VMEM((chunks, LANES, width), bf16),
                pltpu.VMEM((chunks, LANES, width), bf16),
                pltpu.VMEM((n_row, chunks, rows, LANES), i16),
                pltpu.VMEM((n_row, halves, LANES), f32),
                pltpu.VMEM((n_row, rows, LANES), f32),
                pltpu.VMEM((n_row, rows, 2 * LANES), bf16),
                pltpu.VMEM((slots + 1, edge, LANES), f32),
                pltpu.VMEM((slots + 1, edge, LANES), f32),
                pltpu.VMEM((chunks, n_z + 1, rows, LANES), f32),
                pltpu.VMEM((chunks, n_z + 1, rows, LANES), f32),
                pltpu.VMEM((chunks, n_z, rows, LANES), i16),
                pltpu.VMEM((chunks, n_z, halves, LANES), f32),
                pltpu.VMEM((chunks, n_z, rows, LANES), i16),
                pltpu.VMEM((chunks, n_z, halves, LANES), f32),
                pltpu.VMEM((chunks, rows, LANES), f32),
                pltpu.VMEM((n_z + 1, rows, LANES), f32),
                pltpu.VMEM((n_col, halves, LANES), f32),
                pltpu.VMEM((n_col, halves, LANES), f32),
                pltpu.SMEM((n_col,), jnp.int32),
                pltpu.SMEM((slots,), jnp.int32),
                dma((3,)),
                dma((chunks, n_row)),
                dma((chunks, n_row)),
                dma((n_row,)),
                dma((n_row,)),
                dma((chunks, n_z + 1)),
                dma((chunks, n_z + 1)),
                dma((chunks, n_z)),
                dma((chunks, n_z)),
                dma((chunks, n_z)),
                dma((chunks, n_z)),
                dma((n_col,)),
                dma((n_col,)),
            ],
            compiler_params=pltpu.CompilerParams(
                collective_id=0, has_side_effects=True, vmem_limit_bytes=56 * 1024 * 1024
            ),
        )(
            features,
            weight,
            tile_values.reshape(slots, edge, edge),
            tile_ids.reshape(slots, 2).T,
            tile_counts,
        )

    in_specs = (
        P(("col", "row"), None),
        P(),
        P("row", "col", None, None, None),
        P("row", "col", None, None),
        P("row", "col"),
    )
    out_specs = P(("row", "col"), None)
    return jax.shard_map(shards, mesh=mesh, in_specs=in_specs, out_specs=out_specs, check_vma=False)
```

```python
import functools

import jax
import jax.numpy as jnp
from jax import lax
from jax.experimental import pallas as pl
from jax.experimental.pallas import tpu as pltpu
from jax.sharding import PartitionSpec as P

LANES = 128
CORES = 2
GROUP = 32
QMAX = 32767.0
MESH = pl.DeviceIdType.MESH


def quantize(x, peak):
    inverse = QMAX / peak
    return jnp.round(x * inverse).astype(jnp.int32).astype(jnp.int16)


def row_peak(x):
    return jnp.maximum(jnp.max(jnp.abs(x), axis=1, keepdims=True), 1e-30)


def to_row(column):
    wide = jnp.broadcast_to(column, (LANES, LANES))
    eye = lax.broadcasted_iota(jnp.int32, (LANES, LANES), 0) == lax.broadcasted_iota(
        jnp.int32, (LANES, LANES), 1
    )
    return jnp.sum(jnp.where(eye, wide, 0.0), axis=0, keepdims=True)


def to_columns(row):
    return jnp.broadcast_to(row, (LANES, LANES)).T


def kernel(
    n_row, n_col, chunks, slots,
    feat_hbm, w_hbm, tiles_hbm, ids, count,
    out_ref,
    feat, weight, tiles, w_hi, w_lo,
    gq, gs, gscale, rhs, sums, degs,
    xs, xr, zq, zs, zr, zrs, own, mine, ds, dr,
    last, prevs,
    in_sem, g_send, g_recv, gs_send, gs_recv, x_send, x_recv,
    z_send, z_recv, zs_send, zs_recv, d_send, d_recv,
):
    r = lax.axis_index("row")
    c = lax.axis_index("col")
    n_z = n_col // CORES
    z = c // CORES
    core = c % CORES
    other = 1 - core
    rows = feat.shape[0]
    halves = rows // LANES

    barrier = pltpu.get_barrier_semaphore()

    def greet_row(d, _):
        pl.semaphore_signal(barrier, inc=1, device_id=((r + d) % n_row, c), device_id_type=MESH)
        return 0

    def greet_col(d, _):
        pl.semaphore_signal(barrier, inc=1, device_id=(r, (c + d) % n_col), device_id_type=MESH)
        return 0

    lax.fori_loop(1, n_row, greet_row, 0)
    lax.fori_loop(1, n_col, greet_col, 0)

    load_f = pltpu.make_async_copy(feat_hbm, feat, in_sem.at[0])
    load_t = pltpu.make_async_copy(tiles_hbm, tiles, in_sem.at[1])
    load_w = pltpu.make_async_copy(w_hbm, weight, in_sem.at[2])
    load_f.start()
    load_t.start()
    load_w.start()

    for i in range(n_col):
        last[i] = 0

    def link(s, _):
        row = ids[0, s]
        live = s < count[0, 0]
        prevs[s] = last[row]
        for i in range(n_col):
            last[i] = jnp.where(live & (row == i), s + 1, last[i])
        return 0

    load_f.wait()
    values = feat[...]
    peak = row_peak(values)
    for h in range(halves):
        gs[r, h : h + 1, :] = to_row(peak[h * LANES : (h + 1) * LANES] * (1.0 / QMAX))
    for k in range(chunks):
        gq[r, k] = quantize(values[:, k * LANES : (k + 1) * LANES], peak)

    pl.semaphore_wait(barrier, n_row + n_col - 2)

    def scale_copy(d, source):
        return pltpu.make_async_remote_copy(
            src_ref=gs.at[source], dst_ref=gs.at[source],
            send_sem=gs_send.at[d], recv_sem=gs_recv.at[d],
            device_id=((r + d) % n_row, c), device_id_type=MESH,
        )

    def gather_copy(k, d, source):
        return pltpu.make_async_remote_copy(
            src_ref=gq.at[source, k], dst_ref=gq.at[source, k],
            send_sem=g_send.at[k, d], recv_sem=g_recv.at[k, d],
            device_id=((r + d) % n_row, c), device_id_type=MESH,
        )

    def send_scale(d, _):
        scale_copy(d, r).start()
        return 0

    lax.fori_loop(1, n_row, send_scale, 0)

    def send_gather(k):
        def send(d, _):
            gather_copy(k, d, r).start()
            return 0

        lax.fori_loop(1, n_row, send, 0)

    send_gather(0)

    lax.fori_loop(0, slots, link, 0)

    load_t.wait()
    sums[0] = jnp.zeros(sums.shape[1:], jnp.float32)

    def degree_copy(d):
        return pltpu.make_async_remote_copy(
            src_ref=ds.at[(c + d) % n_col], dst_ref=dr.at[d],
            send_sem=d_send.at[d], recv_sem=d_recv.at[d],
            device_id=(r, (c + d) % n_col), device_id_type=MESH,
        )

    def core_copy(k, d):
        return pltpu.make_async_remote_copy(
            src_ref=xs.at[k, d], dst_ref=xr.at[k, d],
            send_sem=x_send.at[k, d], recv_sem=x_recv.at[k, d],
            device_id=(r, z * CORES + other), device_id_type=MESH,
        )

    def z_copies(k, d, target):
        return [
            pltpu.make_async_remote_copy(
                src_ref=source.at[k, d], dst_ref=landing.at[k, d],
                send_sem=sent.at[k, d], recv_sem=landed.at[k, d],
                device_id=(r, target * CORES + core), device_id_type=MESH,
            )
            for source, landing, sent, landed in (
                (zs, zrs, zs_send, zs_recv), (zq, zr, z_send, z_recv),
            )
        ]

    top = n_z - 1
    relays = n_z > 2

    def transmit(k, d, target, value):
        peak = row_peak(value)
        for h in range(halves):
            zs[k, d, h : h + 1, :] = to_row(peak[h * LANES : (h + 1) * LANES] * (1.0 / QMAX))
        zq[k, d] = quantize(value, peak)
        for copy in z_copies(k, d, target):
            copy.start()

    def distance(t):
        return jnp.where((z == top) | (t == n_z), t, n_z - t)

    def relay(k):
        if not relays:
            return

        @pl.when(z == 1)
        def _():
            transmit(k, top - 1, top, xr[k, top - 1] + received(k, n_z))

        @pl.when(z == top - 1)
        def _():
            transmit(k, 2, 0, xr[k, 2] + received(k, n_z + 1))

    def local_block(i):
        j = r * n_col + i - c * n_row
        inside = (j >= 0) & (j < n_row)
        block = rhs[jnp.clip(j, 0, n_row - 1)].astype(jnp.float32)
        block = block[:, :LANES] + block[:, LANES:]
        return sums[last[i]] + jnp.where(inside, block, 0.0)

    def row_sums():
        degs[0] = jnp.zeros(degs.shape[1:], jnp.float32)

        def degree_slot(s, _):
            tile = tiles[s].astype(jnp.float32)
            part = degs[prevs[s]]
            for lane in range(0, tile.shape[1], LANES):
                part = part + tile[:, lane : lane + LANES]
            degs[s + 1] = part
            return 0

        lax.fori_loop(0, slots, degree_slot, 0)

        def degree_block(i, _):
            total = jnp.sum(degs[last[i]], axis=1, keepdims=True)
            for h in range(halves):
                ds[i, h : h + 1, :] = to_row(total[h * LANES : (h + 1) * LANES])
            return 0

        lax.fori_loop(0, n_col, degree_block, 0)

        def send_degree(d, _):
            degree_copy(d).start()
            return 0

        lax.fori_loop(1, n_col, send_degree, 0)

    def split_weight():
        load_w.wait()
        for k in range(chunks):
            part = weight[k * LANES : (k + 1) * LANES, :]
            high = part.astype(jnp.bfloat16)
            w_hi[k] = high
            w_lo[k] = (part - high.astype(jnp.float32)).astype(jnp.bfloat16)

    def received(k, d):
        for copy in z_copies(k, d, jnp.where(z == 0, 1, 0)):
            copy.wait_recv()
        parts = []
        for h in range(halves):
            code = zr[k, d, h * LANES : (h + 1) * LANES]
            scale = to_columns(zrs[k, d, h : h + 1, :])
            parts.append(code.astype(jnp.int32).astype(jnp.float32) * scale)
        return jnp.concatenate(parts, axis=0)

    def project(k):
        def add_z(d, _):
            source = (z + n_z - d) % n_z
            far = ((z == 0) & (source == top)) | ((z == top) & (source == 0))

            @pl.when(jnp.logical_not(far & relays))
            def _():
                own[k] += received(k, d)

            return 0

        lax.fori_loop(1, n_z, add_z, 0)
        total = own[k]
        high = total.astype(jnp.bfloat16)
        low = (total - high.astype(jnp.float32)).astype(jnp.bfloat16)
        dot = functools.partial(jnp.dot, preferred_element_type=jnp.float32)
        out_ref[...] += dot(high, w_hi[k]) + (dot(high, w_lo[k]) + dot(low, w_hi[k]))

    def one_chunk(k, _):
        def wait_gather(d, _):
            gather_copy(k, d, (r + n_row - d) % n_row).wait_recv()
            return 0

        lax.fori_loop(1, n_row, wait_gather, 0)

        @pl.when(k + 1 < chunks)
        def _():
            send_gather(k + 1)

        def decode(j, _):
            value = gq[j, k].astype(jnp.int32).astype(jnp.float32) * gscale[j]
            high = value.astype(jnp.bfloat16)
            rhs[j, :, :LANES] = high
            rhs[j, :, LANES:] = (value - high.astype(jnp.float32)).astype(jnp.bfloat16)
            return 0

        lax.fori_loop(0, n_row, decode, 0)

        def products(g, _):
            for u in range(GROUP):
                s = g * GROUP + u
                both = jnp.dot(tiles[s], rhs[ids[1, s]], preferred_element_type=jnp.float32)
                sums[s + 1] = both[:, :LANES] + both[:, LANES:] + sums[prevs[s]]
            return 0

        lax.fori_loop(0, slots // GROUP, products, 0)

        def hand_over(t, _):
            d = distance(t)
            zz = (z + d) % n_z
            xs[k, d] = local_block(zz * CORES + other)
            core_copy(k, d).start()
            return 0

        lax.fori_loop(1, n_z + 1, hand_over, 0)

        def keep(d, _):
            mine[d] = local_block((z + d) % n_z * CORES + core)
            return 0

        lax.fori_loop(1, n_z + 1, keep, 0)

        @pl.when(k == 0)
        def _():
            split_weight()

        @pl.when(k >= 1)
        def _():
            relay(k - 1)

        @pl.when(k >= 2)
        def _():
            project(k - 2)

        def send_z(t, _):
            d = distance(t)
            zz = (z + d) % n_z
            core_copy(k, d).wait_recv()
            value = mine[d] + xr[k, d]
            from_low = (z == 0) & (zz == top) & relays
            from_high = (z == top) & (zz == 0) & relays
            held = (((z == 1) & (zz == top)) | ((z == top - 1) & (zz == 0))) & relays

            @pl.when(held)
            def _():
                xr[k, d] = value

            @pl.when(jnp.logical_not(held))
            def _():
                slot = jnp.where(from_low, n_z, jnp.where(from_high, n_z + 1, d))
                target = jnp.where(from_low, 1, jnp.where(from_high, top - 1, zz))
                transmit(k, slot, target, value)

            return 0

        lax.fori_loop(1, n_z, send_z, 0)
        core_copy(k, n_z).wait_recv()
        own[k] = mine[n_z] + xr[k, n_z]
        return 0

    row_sums()

    def wait_scale(d, _):
        scale_copy(d, (r + n_row - d) % n_row).wait_recv()
        return 0

    lax.fori_loop(1, n_row, wait_scale, 0)

    def spread_scale(j, _):
        for h in range(halves):
            gscale[j, h * LANES : (h + 1) * LANES, :] = to_columns(gs[j, h : h + 1, :])
        return 0

    lax.fori_loop(0, n_row, spread_scale, 0)
    out_ref[...] = jnp.zeros(out_ref.shape, jnp.float32)
    lax.fori_loop(0, chunks, one_chunk, 0)

    def add_degree(d, total):
        degree_copy(d).wait_recv()
        return total + dr[d]

    degree = lax.fori_loop(1, n_col, add_degree, 1.0 + ds[c])
    root = lax.rsqrt(degree)

    relay(chunks - 1)
    for k in range(max(chunks - 2, 0), chunks):
        project(k)
    for h in range(halves):
        part = slice(h * LANES, (h + 1) * LANES)
        factor = to_columns(root[h : h + 1, :])
        for k in range(chunks):
            cols = slice(k * LANES, (k + 1) * LANES)
            out_ref[part, cols] = jnp.maximum(out_ref[part, cols] * factor, 0.0)

    def drain_row(d, _):
        scale_copy(d, r).wait_send()

        def drain_chunk(k, _):
            gather_copy(k, d, r).wait_send()
            return 0

        lax.fori_loop(0, chunks, drain_chunk, 0)
        return 0

    def drain_degree(d, _):
        degree_copy(d).wait_send()
        return 0

    def drain_core(k, _):
        def drain_x(d, _):
            core_copy(k, d).wait_send()
            return 0

        lax.fori_loop(1, n_z + 1, drain_x, 0)

        def drain_z(d, _):
            target = (z + d) % n_z
            from_low = (z == 0) & (target == top) & relays
            from_high = (z == top) & (target == 0) & relays
            slot = jnp.where(from_low, n_z, jnp.where(from_high, n_z + 1, d))
            for copy in z_copies(k, slot, target):
                copy.wait_send()
            return 0

        lax.fori_loop(1, n_z, drain_z, 0)
        return 0

    lax.fori_loop(1, n_row, drain_row, 0)
    lax.fori_loop(1, n_col, drain_degree, 0)
    lax.fori_loop(0, chunks, drain_core, 0)


def solution(mesh):
    n_row, n_col = mesh.shape["row"], mesh.shape["col"]
    n_z = n_col // CORES

    def shards(features, weight, tile_values, tile_ids, tile_counts):
        rows, width = features.shape
        slots, edge = tile_values.shape[2], tile_values.shape[3]
        chunks = width // LANES
        halves = rows // LANES
        f32, bf16, i16 = jnp.float32, jnp.bfloat16, jnp.int16
        dma = pltpu.SemaphoreType.DMA
        hbm = pl.BlockSpec(memory_space=pl.ANY)
        smem = pl.BlockSpec(memory_space=pltpu.SMEM)
        vmem = pl.BlockSpec(memory_space=pltpu.VMEM)
        return pl.pallas_call(
            functools.partial(kernel, n_row, n_col, chunks, slots),
            out_shape=jax.ShapeDtypeStruct((rows, width), f32),
            in_specs=[hbm, hbm, hbm, smem, smem],
            out_specs=vmem,
            scratch_shapes=[
                pltpu.VMEM((rows, width), f32),
                pltpu.VMEM((width, width), f32),
                pltpu.VMEM((slots, edge, edge), bf16),
                pltpu.VMEM((chunks, LANES, width), bf16),
                pltpu.VMEM((chunks, LANES, width), bf16),
                pltpu.VMEM((n_row, chunks, rows, LANES), i16),
                pltpu.VMEM((n_row, halves, LANES), f32),
                pltpu.VMEM((n_row, rows, LANES), f32),
                pltpu.VMEM((n_row, rows, 2 * LANES), bf16),
                pltpu.VMEM((slots + 1, edge, LANES), f32),
                pltpu.VMEM((slots + 1, edge, LANES), f32),
                pltpu.VMEM((chunks, n_z + 1, rows, LANES), f32),
                pltpu.VMEM((chunks, n_z + 1, rows, LANES), f32),
                pltpu.VMEM((chunks, n_z + 2, rows, LANES), i16),
                pltpu.VMEM((chunks, n_z + 2, halves, LANES), f32),
                pltpu.VMEM((chunks, n_z + 2, rows, LANES), i16),
                pltpu.VMEM((chunks, n_z + 2, halves, LANES), f32),
                pltpu.VMEM((chunks, rows, LANES), f32),
                pltpu.VMEM((n_z + 1, rows, LANES), f32),
                pltpu.VMEM((n_col, halves, LANES), f32),
                pltpu.VMEM((n_col, halves, LANES), f32),
                pltpu.SMEM((n_col,), jnp.int32),
                pltpu.SMEM((slots,), jnp.int32),
                dma((3,)),
                dma((chunks, n_row)),
                dma((chunks, n_row)),
                dma((n_row,)),
                dma((n_row,)),
                dma((chunks, n_z + 1)),
                dma((chunks, n_z + 1)),
                dma((chunks, n_z + 2)),
                dma((chunks, n_z + 2)),
                dma((chunks, n_z + 2)),
                dma((chunks, n_z + 2)),
                dma((n_col,)),
                dma((n_col,)),
            ],
            compiler_params=pltpu.CompilerParams(
                collective_id=0, has_side_effects=True, vmem_limit_bytes=56 * 1024 * 1024
            ),
        )(
            features,
            weight,
            tile_values.reshape(slots, edge, edge),
            tile_ids.reshape(slots, 2).T,
            tile_counts,
        )

    in_specs = (
        P(("col", "row"), None),
        P(),
        P("row", "col", None, None, None),
        P("row", "col", None, None),
        P("row", "col"),
    )
    out_specs = P(("row", "col"), None)
    return jax.shard_map(shards, mesh=mesh, in_specs=in_specs, out_specs=out_specs, check_vma=False)
```

```python
import functools

import jax
import jax.numpy as jnp
from jax import lax
from jax.experimental import pallas as pl
from jax.experimental.pallas import tpu as pltpu
from jax.sharding import PartitionSpec as P

LANES = 128
CORES = 2
GROUP = 32
QMAX = 32767.0
MESH = pl.DeviceIdType.MESH


def quantize(x, peak):
    inverse = QMAX / peak
    return jnp.round(x * inverse).astype(jnp.int32).astype(jnp.int16)


def row_peak(x):
    return jnp.maximum(jnp.max(jnp.abs(x), axis=1, keepdims=True), 1e-30)


def to_row(column):
    wide = jnp.broadcast_to(column, (LANES, LANES))
    eye = lax.broadcasted_iota(jnp.int32, (LANES, LANES), 0) == lax.broadcasted_iota(
        jnp.int32, (LANES, LANES), 1
    )
    return jnp.sum(jnp.where(eye, wide, 0.0), axis=0, keepdims=True)


def to_columns(row):
    return jnp.broadcast_to(row, (LANES, LANES)).T


def kernel(
    n_row, n_col, chunks, slots,
    feat_hbm, w_hbm, tiles_hbm, ids, count,
    out_ref,
    feat, weight, tiles, w_hi, w_lo,
    gq, gs, gscale, rhs, sums, degs,
    xs, xr, zq, zs, zr, zrs, own, kept, ds, dr,
    last, prevs,
    in_sem, g_send, g_recv, gs_send, gs_recv, x_send, x_recv,
    z_send, z_recv, zs_send, zs_recv, d_send, d_recv,
):
    r = lax.axis_index("row")
    c = lax.axis_index("col")
    n_z = n_col // CORES
    z = c // CORES
    core = c % CORES
    other = 1 - core
    rows = feat.shape[0]
    halves = rows // LANES

    barrier = pltpu.get_barrier_semaphore()

    def greet_row(d, _):
        pl.semaphore_signal(barrier, inc=1, device_id=((r + d) % n_row, c), device_id_type=MESH)
        return 0

    def greet_col(d, _):
        pl.semaphore_signal(barrier, inc=1, device_id=(r, (c + d) % n_col), device_id_type=MESH)
        return 0

    lax.fori_loop(1, n_row, greet_row, 0)
    lax.fori_loop(1, n_col, greet_col, 0)

    load_f = pltpu.make_async_copy(feat_hbm, feat, in_sem.at[0])
    load_t = pltpu.make_async_copy(tiles_hbm, tiles, in_sem.at[1])
    load_w = pltpu.make_async_copy(w_hbm, weight, in_sem.at[2])
    load_f.start()
    load_t.start()
    load_w.start()

    for i in range(n_col):
        last[i] = i

    def link(s, _):
        row = ids[0, s]
        live = s < count[0, 0]
        prevs[s] = last[row]
        for i in range(n_col):
            last[i] = jnp.where(live & (row == i), n_col + s, last[i])
        return 0

    load_f.wait()
    values = feat[...]
    peak = row_peak(values)
    for h in range(halves):
        gs[r, h : h + 1, :] = to_row(peak[h * LANES : (h + 1) * LANES] * (1.0 / QMAX))
    for k in range(chunks):
        gq[r, k] = quantize(values[:, k * LANES : (k + 1) * LANES], peak)

    pl.semaphore_wait(barrier, n_row + n_col - 2)

    def scale_copy(d, source):
        return pltpu.make_async_remote_copy(
            src_ref=gs.at[source], dst_ref=gs.at[source],
            send_sem=gs_send.at[d], recv_sem=gs_recv.at[d],
            device_id=((r + d) % n_row, c), device_id_type=MESH,
        )

    def gather_copy(k, d, source):
        return pltpu.make_async_remote_copy(
            src_ref=gq.at[source, k], dst_ref=gq.at[source, k],
            send_sem=g_send.at[k, d], recv_sem=g_recv.at[k, d],
            device_id=((r + d) % n_row, c), device_id_type=MESH,
        )

    def send_scale(d, _):
        scale_copy(d, r).start()
        return 0

    lax.fori_loop(1, n_row, send_scale, 0)

    def send_gather(k):
        def send(d, _):
            gather_copy(k, d, r).start()
            return 0

        lax.fori_loop(1, n_row, send, 0)

    send_gather(0)

    lax.fori_loop(0, slots, link, 0)

    load_t.wait()

    def degree_copy(d):
        return pltpu.make_async_remote_copy(
            src_ref=ds.at[(c + d) % n_col], dst_ref=dr.at[d],
            send_sem=d_send.at[d], recv_sem=d_recv.at[d],
            device_id=(r, (c + d) % n_col), device_id_type=MESH,
        )

    def core_copy(k, d):
        return pltpu.make_async_remote_copy(
            src_ref=xs.at[k, d], dst_ref=xr.at[k, d],
            send_sem=x_send.at[k, d], recv_sem=x_recv.at[k, d],
            device_id=(r, z * CORES + other), device_id_type=MESH,
        )

    def z_copies(k, d, target):
        return [
            pltpu.make_async_remote_copy(
                src_ref=source.at[k, d], dst_ref=landing.at[k, d],
                send_sem=sent.at[k, d], recv_sem=landed.at[k, d],
                device_id=(r, target * CORES + core), device_id_type=MESH,
            )
            for source, landing, sent, landed in (
                (zs, zrs, zs_send, zs_recv), (zq, zr, z_send, z_recv),
            )
        ]

    top = n_z - 1
    relays = n_z > 2

    def encode(k, d, value):
        peak = row_peak(value)
        for h in range(halves):
            zs[k, d, h : h + 1, :] = to_row(peak[h * LANES : (h + 1) * LANES] * (1.0 / QMAX))
        zq[k, d] = quantize(value, peak)

    def transmit(k, d, target, value):
        encode(k, d, value)
        for copy in z_copies(k, d, target):
            copy.start()

    def distance(t):
        return jnp.where((z == top) | (t == n_z), t, n_z - t)

    def relay(k):
        if not relays:
            return

        @pl.when(z == 1)
        def _():
            transmit(k, top - 1, top, kept[k, top - 1] + received(k, n_z))

        @pl.when(z == top - 1)
        def _():
            transmit(k, 2, 0, kept[k, 2] + received(k, n_z + 1))

    def row_sums():
        for i in range(n_col):
            degs[i] = jnp.zeros(degs.shape[1:], jnp.float32)
            sums[i] = jnp.zeros(sums.shape[1:], jnp.float32)

        def degree_slot(s, _):
            tile = tiles[s].astype(jnp.float32)
            part = degs[prevs[s]]
            for lane in range(0, tile.shape[1], LANES):
                part = part + tile[:, lane : lane + LANES]
            degs[n_col + s] = part
            return 0

        lax.fori_loop(0, slots, degree_slot, 0, unroll=8)

        def degree_block(i, _):
            total = jnp.sum(degs[last[i]], axis=1, keepdims=True)
            for h in range(halves):
                ds[i, h : h + 1, :] = to_row(total[h * LANES : (h + 1) * LANES])
            return 0

        lax.fori_loop(0, n_col, degree_block, 0, unroll=8)

        def send_degree(d, _):
            degree_copy(d).start()
            return 0

        lax.fori_loop(1, n_col, send_degree, 0)

    def split_weight():
        load_w.wait()
        for k in range(chunks):
            part = weight[k * LANES : (k + 1) * LANES, :]
            high = part.astype(jnp.bfloat16)
            w_hi[k] = high
            w_lo[k] = (part - high.astype(jnp.float32)).astype(jnp.bfloat16)

    def arrive(k, d):
        for copy in z_copies(k, d, jnp.where(z == 0, 1, 0)):
            copy.wait_recv()

    def decoded(k, d):
        parts = []
        for h in range(halves):
            code = zr[k, d, h * LANES : (h + 1) * LANES]
            scale = to_columns(zrs[k, d, h : h + 1, :])
            parts.append(code.astype(jnp.int32).astype(jnp.float32) * scale)
        return jnp.concatenate(parts, axis=0)

    def received(k, d):
        arrive(k, d)
        return decoded(k, d)

    def project(k):
        def is_far(d):
            source = (z + n_z - d) % n_z
            return (((z == 0) & (source == top)) | ((z == top) & (source == 0))) & relays

        def wait_z(d, _):
            @pl.when(jnp.logical_not(is_far(d)))
            def _():
                arrive(k, d)

            return 0

        def add_z(d, total):
            far = is_far(d)
            return total + jnp.where(far, 0.0, decoded(k, jnp.where(far, 2, d)))

        lax.fori_loop(1, n_z, wait_z, 0)
        total = lax.fori_loop(1, n_z, add_z, own[k], unroll=min(n_z - 1, 4))
        high = total.astype(jnp.bfloat16)
        low = (total - high.astype(jnp.float32)).astype(jnp.bfloat16)
        dot = functools.partial(jnp.dot, preferred_element_type=jnp.float32)
        out_ref[...] += dot(high, w_hi[k]) + (dot(high, w_lo[k]) + dot(low, w_hi[k]))

    def one_chunk(k, _):
        def wait_gather(d, _):
            gather_copy(k, d, (r + n_row - d) % n_row).wait_recv()
            return 0

        lax.fori_loop(1, n_row, wait_gather, 0)

        @pl.when(k + 1 < chunks)
        def _():
            send_gather(k + 1)

        def decode(j, _):
            value = gq[j, k].astype(jnp.int32).astype(jnp.float32) * gscale[j]
            high = value.astype(jnp.bfloat16)
            rhs[j, :, :LANES] = high
            rhs[j, :, LANES:] = (value - high.astype(jnp.float32)).astype(jnp.bfloat16)
            block = c * n_row + j - r * n_col
            inside = (block >= 0) & (block < n_col)
            sums[jnp.where(inside, block, n_col + slots)] = value
            return 0

        lax.fori_loop(0, n_row, decode, 0, unroll=4)

        def products(g, _):
            for u in range(GROUP):
                s = g * GROUP + u
                both = jnp.dot(tiles[s], rhs[ids[1, s]], preferred_element_type=jnp.float32)
                sums[n_col + s] = both[:, :LANES] + both[:, LANES:] + sums[prevs[s]]
            return 0

        lax.fori_loop(0, slots // GROUP, products, 0)

        def hand_over(t, _):
            d = distance(t)
            zz = (z + d) % n_z
            xs[k, d] = sums[last[zz * CORES + other]]
            core_copy(k, d).start()
            return 0

        lax.fori_loop(1, n_z + 1, hand_over, 0)

        @pl.when(k == 0)
        def _():
            split_weight()

        @pl.when(k >= 1)
        def _():
            relay(k - 1)

        @pl.when(k >= 2)
        def _():
            project(k - 2)

        def route(t):
            d = distance(t)
            zz = (z + d) % n_z
            from_low = (z == 0) & (zz == top) & relays
            from_high = (z == top) & (zz == 0) & relays
            held = (((z == 1) & (zz == top)) | ((z == top - 1) & (zz == 0))) & relays
            slot = jnp.where(from_low, n_z, jnp.where(from_high, n_z + 1, d))
            target = jnp.where(from_low, 1, jnp.where(from_high, top - 1, zz))
            return d, zz, slot, target, held

        def wait_core(t, _):
            core_copy(k, t).wait_recv()
            return 0

        lax.fori_loop(1, n_z + 1, wait_core, 0)

        def code_z(t, _):
            d, zz, slot, target, held = route(t)
            value = sums[last[zz * CORES + core]] + xr[k, d]
            kept[k, d] = value
            encode(k, slot, value)
            return 0

        def send_z(t, _):
            d, zz, slot, target, held = route(t)

            @pl.when(jnp.logical_not(held))
            def _():
                for copy in z_copies(k, slot, target):
                    copy.start()

            return 0

        code_z(1, 0)
        send_z(1, 0)
        lax.fori_loop(2, n_z, code_z, 0, unroll=min(n_z - 2, 4))
        lax.fori_loop(2, n_z, send_z, 0)
        own[k] = sums[last[c]] + xr[k, n_z]
        return 0

    row_sums()

    def wait_scale(d, _):
        scale_copy(d, (r + n_row - d) % n_row).wait_recv()
        return 0

    lax.fori_loop(1, n_row, wait_scale, 0)

    def spread_scale(j, _):
        for h in range(halves):
            gscale[j, h * LANES : (h + 1) * LANES, :] = to_columns(gs[j, h : h + 1, :])
        return 0

    lax.fori_loop(0, n_row, spread_scale, 0, unroll=4)
    out_ref[...] = jnp.zeros(out_ref.shape, jnp.float32)
    lax.fori_loop(0, chunks, one_chunk, 0)

    def add_degree(d, total):
        degree_copy(d).wait_recv()
        return total + dr[d]

    degree = lax.fori_loop(1, n_col, add_degree, 1.0 + ds[c])
    root = lax.rsqrt(degree)

    relay(chunks - 1)
    for k in range(max(chunks - 2, 0), chunks):
        project(k)
    for h in range(halves):
        part = slice(h * LANES, (h + 1) * LANES)
        factor = to_columns(root[h : h + 1, :])
        for k in range(chunks):
            cols = slice(k * LANES, (k + 1) * LANES)
            out_ref[part, cols] = jnp.maximum(out_ref[part, cols] * factor, 0.0)

    def drain_row(d, _):
        scale_copy(d, r).wait_send()

        def drain_chunk(k, _):
            gather_copy(k, d, r).wait_send()
            return 0

        lax.fori_loop(0, chunks, drain_chunk, 0)
        return 0

    def drain_degree(d, _):
        degree_copy(d).wait_send()
        return 0

    def drain_core(k, _):
        def drain_x(d, _):
            core_copy(k, d).wait_send()
            return 0

        lax.fori_loop(1, n_z + 1, drain_x, 0)

        def drain_z(d, _):
            target = (z + d) % n_z
            from_low = (z == 0) & (target == top) & relays
            from_high = (z == top) & (target == 0) & relays
            slot = jnp.where(from_low, n_z, jnp.where(from_high, n_z + 1, d))
            for copy in z_copies(k, slot, target):
                copy.wait_send()
            return 0

        lax.fori_loop(1, n_z, drain_z, 0)
        return 0

    lax.fori_loop(1, n_row, drain_row, 0)
    lax.fori_loop(1, n_col, drain_degree, 0)
    lax.fori_loop(0, chunks, drain_core, 0)


def solution(mesh):
    n_row, n_col = mesh.shape["row"], mesh.shape["col"]
    n_z = n_col // CORES

    def shards(features, weight, tile_values, tile_ids, tile_counts):
        rows, width = features.shape
        slots, edge = tile_values.shape[2], tile_values.shape[3]
        chunks = width // LANES
        halves = rows // LANES
        f32, bf16, i16 = jnp.float32, jnp.bfloat16, jnp.int16
        dma = pltpu.SemaphoreType.DMA
        hbm = pl.BlockSpec(memory_space=pl.ANY)
        smem = pl.BlockSpec(memory_space=pltpu.SMEM)
        vmem = pl.BlockSpec(memory_space=pltpu.VMEM)
        return pl.pallas_call(
            functools.partial(kernel, n_row, n_col, chunks, slots),
            out_shape=jax.ShapeDtypeStruct((rows, width), f32),
            in_specs=[hbm, hbm, hbm, smem, smem],
            out_specs=vmem,
            scratch_shapes=[
                pltpu.VMEM((rows, width), f32),
                pltpu.VMEM((width, width), f32),
                pltpu.VMEM((slots, edge, edge), bf16),
                pltpu.VMEM((chunks, LANES, width), bf16),
                pltpu.VMEM((chunks, LANES, width), bf16),
                pltpu.VMEM((n_row, chunks, rows, LANES), i16),
                pltpu.VMEM((n_row, halves, LANES), f32),
                pltpu.VMEM((n_row, rows, LANES), f32),
                pltpu.VMEM((n_row, rows, 2 * LANES), bf16),
                pltpu.VMEM((n_col + slots + 1, edge, LANES), f32),
                pltpu.VMEM((n_col + slots + 1, edge, LANES), f32),
                pltpu.VMEM((chunks, n_z + 1, rows, LANES), f32),
                pltpu.VMEM((chunks, n_z + 1, rows, LANES), f32),
                pltpu.VMEM((chunks, n_z + 2, rows, LANES), i16),
                pltpu.VMEM((chunks, n_z + 2, halves, LANES), f32),
                pltpu.VMEM((chunks, n_z + 2, rows, LANES), i16),
                pltpu.VMEM((chunks, n_z + 2, halves, LANES), f32),
                pltpu.VMEM((chunks, rows, LANES), f32),
                pltpu.VMEM((chunks, n_z, rows, LANES), f32),
                pltpu.VMEM((n_col, halves, LANES), f32),
                pltpu.VMEM((n_col, halves, LANES), f32),
                pltpu.SMEM((n_col,), jnp.int32),
                pltpu.SMEM((slots,), jnp.int32),
                dma((3,)),
                dma((chunks, n_row)),
                dma((chunks, n_row)),
                dma((n_row,)),
                dma((n_row,)),
                dma((chunks, n_z + 1)),
                dma((chunks, n_z + 1)),
                dma((chunks, n_z + 2)),
                dma((chunks, n_z + 2)),
                dma((chunks, n_z + 2)),
                dma((chunks, n_z + 2)),
                dma((n_col,)),
                dma((n_col,)),
            ],
            compiler_params=pltpu.CompilerParams(
                collective_id=0, has_side_effects=True, vmem_limit_bytes=56 * 1024 * 1024
            ),
        )(
            features,
            weight,
            tile_values.reshape(slots, edge, edge),
            tile_ids.reshape(slots, 2).T,
            tile_counts,
        )

    in_specs = (
        P(("col", "row"), None),
        P(),
        P("row", "col", None, None, None),
        P("row", "col", None, None),
        P("row", "col"),
    )
    out_specs = P(("row", "col"), None)
    return jax.shard_map(shards, mesh=mesh, in_specs=in_specs, out_specs=out_specs, check_vma=False)
```

```python
import functools

import jax
import jax.numpy as jnp
from jax import lax
from jax.experimental import pallas as pl
from jax.experimental.pallas import tpu as pltpu
from jax.sharding import PartitionSpec as P

LANES = 128
CORES = 2
GROUP = 32
AHEAD = 2
QMAX = 32767.0
MESH = pl.DeviceIdType.MESH


def quantize(x, peak):
    inverse = QMAX / peak
    return jnp.round(x * inverse).astype(jnp.int32).astype(jnp.int16)


def row_peak(x):
    return jnp.maximum(jnp.max(jnp.abs(x), axis=1, keepdims=True), 1e-30)


def to_row(column):
    wide = jnp.broadcast_to(column, (LANES, LANES))
    eye = lax.broadcasted_iota(jnp.int32, (LANES, LANES), 0) == lax.broadcasted_iota(
        jnp.int32, (LANES, LANES), 1
    )
    return jnp.sum(jnp.where(eye, wide, 0.0), axis=0, keepdims=True)


def to_columns(row):
    return jnp.broadcast_to(row, (LANES, LANES)).T


def kernel(
    n_row, n_col, chunks, slots,
    feat_hbm, w_hbm, tiles_hbm, ids, count,
    out_ref,
    feat, weight, tiles, w_hi, w_lo,
    gq, gs, gscale, rhs, sums, degs,
    xs, xr, zq, zs, zr, zrs, own, kept, ds, dr,
    last, prevs,
    in_sem, g_send, g_recv, gs_send, gs_recv, x_send, x_recv,
    z_send, z_recv, zs_send, zs_recv, d_send, d_recv,
):
    r = lax.axis_index("row")
    c = lax.axis_index("col")
    n_z = n_col // CORES
    z = c // CORES
    core = c % CORES
    other = 1 - core
    rows = feat.shape[0]
    halves = rows // LANES

    barrier = pltpu.get_barrier_semaphore()

    def greet_row(d, _):
        pl.semaphore_signal(barrier, inc=1, device_id=((r + d) % n_row, c), device_id_type=MESH)
        return 0

    def greet_col(d, _):
        pl.semaphore_signal(barrier, inc=1, device_id=(r, (c + d) % n_col), device_id_type=MESH)
        return 0

    lax.fori_loop(1, n_row, greet_row, 0)
    lax.fori_loop(1, n_col, greet_col, 0)

    load_f = pltpu.make_async_copy(feat_hbm, feat, in_sem.at[0])
    load_t = pltpu.make_async_copy(tiles_hbm, tiles, in_sem.at[1])
    load_w = pltpu.make_async_copy(w_hbm, weight, in_sem.at[2])
    load_f.start()
    load_t.start()
    load_w.start()

    for i in range(n_col):
        last[i] = i

    def link(s, _):
        row = ids[0, s]
        live = s < count[0, 0]
        prevs[s] = last[row]
        for i in range(n_col):
            last[i] = jnp.where(live & (row == i), n_col + s, last[i])
        return 0

    load_f.wait()
    values = feat[...]
    peak = row_peak(values)
    for h in range(halves):
        gs[r, h : h + 1, :] = to_row(peak[h * LANES : (h + 1) * LANES] * (1.0 / QMAX))
    for k in range(chunks):
        gq[r, k] = quantize(values[:, k * LANES : (k + 1) * LANES], peak)

    pl.semaphore_wait(barrier, n_row + n_col - 2)

    def scale_copy(d, source):
        return pltpu.make_async_remote_copy(
            src_ref=gs.at[source], dst_ref=gs.at[source],
            send_sem=gs_send.at[d], recv_sem=gs_recv.at[d],
            device_id=((r + d) % n_row, c), device_id_type=MESH,
        )

    def gather_copy(k, d, source):
        return pltpu.make_async_remote_copy(
            src_ref=gq.at[source, k], dst_ref=gq.at[source, k],
            send_sem=g_send.at[k, d], recv_sem=g_recv.at[k, d],
            device_id=((r + d) % n_row, c), device_id_type=MESH,
        )

    def send_scale(d, _):
        scale_copy(d, r).start()
        return 0

    lax.fori_loop(1, n_row, send_scale, 0)

    def send_gather(k):
        def send(d, _):
            gather_copy(k, d, r).start()
            return 0

        lax.fori_loop(1, n_row, send, 0)

    for k in range(min(AHEAD, chunks)):
        send_gather(k)

    lax.fori_loop(0, slots, link, 0)

    load_t.wait()

    def degree_copy(d):
        return pltpu.make_async_remote_copy(
            src_ref=ds.at[(c + d) % n_col], dst_ref=dr.at[d],
            send_sem=d_send.at[d], recv_sem=d_recv.at[d],
            device_id=(r, (c + d) % n_col), device_id_type=MESH,
        )

    def core_copy(k, d):
        return pltpu.make_async_remote_copy(
            src_ref=xs.at[k, d], dst_ref=xr.at[k, d],
            send_sem=x_send.at[k, d], recv_sem=x_recv.at[k, d],
            device_id=(r, z * CORES + other), device_id_type=MESH,
        )

    def z_copies(k, d, target):
        return [
            pltpu.make_async_remote_copy(
                src_ref=source.at[k, d], dst_ref=landing.at[k, d],
                send_sem=sent.at[k, d], recv_sem=landed.at[k, d],
                device_id=(r, target * CORES + core), device_id_type=MESH,
            )
            for source, landing, sent, landed in (
                (zs, zrs, zs_send, zs_recv), (zq, zr, z_send, z_recv),
            )
        ]

    top = n_z - 1
    relays = n_z > 2

    def encode(k, d, value):
        peak = row_peak(value)
        for h in range(halves):
            zs[k, d, h : h + 1, :] = to_row(peak[h * LANES : (h + 1) * LANES] * (1.0 / QMAX))
        zq[k, d] = quantize(value, peak)

    def transmit(k, d, target, value):
        encode(k, d, value)
        for copy in z_copies(k, d, target):
            copy.start()

    def distance(t):
        return jnp.where((z == top) | (t == n_z), t, n_z - t)

    def relay(k):
        if not relays:
            return

        @pl.when(z == 1)
        def _():
            transmit(k, top - 1, top, kept[k, top - 1] + received(k, n_z))

        @pl.when(z == top - 1)
        def _():
            transmit(k, 2, 0, kept[k, 2] + received(k, n_z + 1))

    def row_sums():
        for i in range(n_col):
            degs[i] = jnp.zeros(degs.shape[1:], jnp.float32)
            sums[i] = jnp.zeros(sums.shape[1:], jnp.float32)

        def degree_slot(s, _):
            tile = tiles[s].astype(jnp.float32)
            part = degs[prevs[s]]
            for lane in range(0, tile.shape[1], LANES):
                part = part + tile[:, lane : lane + LANES]
            degs[n_col + s] = part
            return 0

        lax.fori_loop(0, slots, degree_slot, 0, unroll=8)

        def degree_block(i, _):
            total = jnp.sum(degs[last[i]], axis=1, keepdims=True)
            for h in range(halves):
                ds[i, h : h + 1, :] = to_row(total[h * LANES : (h + 1) * LANES])
            return 0

        lax.fori_loop(0, n_col, degree_block, 0, unroll=8)

        def send_degree(d, _):
            degree_copy(d).start()
            return 0

        lax.fori_loop(1, n_col, send_degree, 0)

    def split_weight():
        load_w.wait()
        for k in range(chunks):
            part = weight[k * LANES : (k + 1) * LANES, :]
            high = part.astype(jnp.bfloat16)
            w_hi[k] = high
            w_lo[k] = (part - high.astype(jnp.float32)).astype(jnp.bfloat16)

    def arrive(k, d):
        for copy in z_copies(k, d, jnp.where(z == 0, 1, 0)):
            copy.wait_recv()

    def decoded(k, d):
        parts = []
        for h in range(halves):
            code = zr[k, d, h * LANES : (h + 1) * LANES]
            scale = to_columns(zrs[k, d, h : h + 1, :])
            parts.append(code.astype(jnp.int32).astype(jnp.float32) * scale)
        return jnp.concatenate(parts, axis=0)

    def received(k, d):
        arrive(k, d)
        return decoded(k, d)

    def project(k):
        def is_far(d):
            source = (z + n_z - d) % n_z
            return (((z == 0) & (source == top)) | ((z == top) & (source == 0))) & relays

        def wait_z(d, _):
            @pl.when(jnp.logical_not(is_far(d)))
            def _():
                arrive(k, d)

            return 0

        def add_z(d, total):
            far = is_far(d)
            return total + jnp.where(far, 0.0, decoded(k, jnp.where(far, 2, d)))

        lax.fori_loop(1, n_z, wait_z, 0)
        total = lax.fori_loop(1, n_z, add_z, own[k], unroll=min(n_z - 1, 4))
        high = total.astype(jnp.bfloat16)
        low = (total - high.astype(jnp.float32)).astype(jnp.bfloat16)
        dot = functools.partial(jnp.dot, preferred_element_type=jnp.float32)
        out_ref[...] += dot(high, w_hi[k]) + (dot(high, w_lo[k]) + dot(low, w_hi[k]))

    def one_chunk(k, _):
        def wait_gather(d, _):
            gather_copy(k, d, (r + n_row - d) % n_row).wait_recv()
            return 0

        lax.fori_loop(1, n_row, wait_gather, 0)

        @pl.when(k + AHEAD < chunks)
        def _():
            send_gather(k + AHEAD)

        def decode(j, _):
            value = gq[j, k].astype(jnp.int32).astype(jnp.float32) * gscale[j]
            high = value.astype(jnp.bfloat16)
            rhs[j, :, :LANES] = high
            rhs[j, :, LANES:] = (value - high.astype(jnp.float32)).astype(jnp.bfloat16)
            block = c * n_row + j - r * n_col
            inside = (block >= 0) & (block < n_col)
            sums[jnp.where(inside, block, n_col + slots)] = value
            return 0

        lax.fori_loop(0, n_row, decode, 0, unroll=4)

        def products(g, _):
            for u in range(GROUP):
                s = g * GROUP + u
                both = jnp.dot(tiles[s], rhs[ids[1, s]], preferred_element_type=jnp.float32)
                sums[n_col + s] = both[:, :LANES] + both[:, LANES:] + sums[prevs[s]]
            return 0

        lax.fori_loop(0, slots // GROUP, products, 0)

        def hand_over(t, _):
            d = distance(t)
            zz = (z + d) % n_z
            xs[k, d] = sums[last[zz * CORES + other]]
            core_copy(k, d).start()
            return 0

        lax.fori_loop(1, n_z + 1, hand_over, 0)

        @pl.when(k == 0)
        def _():
            split_weight()

        @pl.when(k >= 1)
        def _():
            relay(k - 1)

        @pl.when(k >= 2)
        def _():
            project(k - 2)

        def route(t):
            d = distance(t)
            zz = (z + d) % n_z
            from_low = (z == 0) & (zz == top) & relays
            from_high = (z == top) & (zz == 0) & relays
            held = (((z == 1) & (zz == top)) | ((z == top - 1) & (zz == 0))) & relays
            slot = jnp.where(from_low, n_z, jnp.where(from_high, n_z + 1, d))
            target = jnp.where(from_low, 1, jnp.where(from_high, top - 1, zz))
            return d, zz, slot, target, held

        def wait_core(t, _):
            core_copy(k, t).wait_recv()
            return 0

        lax.fori_loop(1, n_z + 1, wait_core, 0)

        def code_z(t, _):
            d, zz, slot, target, held = route(t)
            value = sums[last[zz * CORES + core]] + xr[k, d]
            kept[k, d] = value
            encode(k, slot, value)
            return 0

        def send_z(t, _):
            d, zz, slot, target, held = route(t)

            @pl.when(jnp.logical_not(held))
            def _():
                for copy in z_copies(k, slot, target):
                    copy.start()

            return 0

        code_z(1, 0)
        send_z(1, 0)
        lax.fori_loop(2, n_z, code_z, 0, unroll=min(n_z - 2, 4))
        lax.fori_loop(2, n_z, send_z, 0)
        own[k] = sums[last[c]] + xr[k, n_z]
        return 0

    row_sums()

    def wait_scale(d, _):
        scale_copy(d, (r + n_row - d) % n_row).wait_recv()
        return 0

    lax.fori_loop(1, n_row, wait_scale, 0)

    def spread_scale(j, _):
        for h in range(halves):
            gscale[j, h * LANES : (h + 1) * LANES, :] = to_columns(gs[j, h : h + 1, :])
        return 0

    lax.fori_loop(0, n_row, spread_scale, 0, unroll=4)
    out_ref[...] = jnp.zeros(out_ref.shape, jnp.float32)
    lax.fori_loop(0, chunks, one_chunk, 0)

    def add_degree(d, total):
        degree_copy(d).wait_recv()
        return total + dr[d]

    degree = lax.fori_loop(1, n_col, add_degree, 1.0 + ds[c])
    root = lax.rsqrt(degree)

    relay(chunks - 1)
    for k in range(max(chunks - 2, 0), chunks):
        project(k)
    for h in range(halves):
        part = slice(h * LANES, (h + 1) * LANES)
        factor = to_columns(root[h : h + 1, :])
        for k in range(chunks):
            cols = slice(k * LANES, (k + 1) * LANES)
            out_ref[part, cols] = jnp.maximum(out_ref[part, cols] * factor, 0.0)

    def drain_row(d, _):
        scale_copy(d, r).wait_send()

        def drain_chunk(k, _):
            gather_copy(k, d, r).wait_send()
            return 0

        lax.fori_loop(0, chunks, drain_chunk, 0)
        return 0

    def drain_degree(d, _):
        degree_copy(d).wait_send()
        return 0

    def drain_core(k, _):
        def drain_x(d, _):
            core_copy(k, d).wait_send()
            return 0

        lax.fori_loop(1, n_z + 1, drain_x, 0)

        def drain_z(d, _):
            target = (z + d) % n_z
            from_low = (z == 0) & (target == top) & relays
            from_high = (z == top) & (target == 0) & relays
            slot = jnp.where(from_low, n_z, jnp.where(from_high, n_z + 1, d))
            for copy in z_copies(k, slot, target):
                copy.wait_send()
            return 0

        lax.fori_loop(1, n_z, drain_z, 0)
        return 0

    lax.fori_loop(1, n_row, drain_row, 0)
    lax.fori_loop(1, n_col, drain_degree, 0)
    lax.fori_loop(0, chunks, drain_core, 0)


def solution(mesh):
    n_row, n_col = mesh.shape["row"], mesh.shape["col"]
    n_z = n_col // CORES

    def shards(features, weight, tile_values, tile_ids, tile_counts):
        rows, width = features.shape
        slots, edge = tile_values.shape[2], tile_values.shape[3]
        chunks = width // LANES
        halves = rows // LANES
        f32, bf16, i16 = jnp.float32, jnp.bfloat16, jnp.int16
        dma = pltpu.SemaphoreType.DMA
        hbm = pl.BlockSpec(memory_space=pl.ANY)
        smem = pl.BlockSpec(memory_space=pltpu.SMEM)
        vmem = pl.BlockSpec(memory_space=pltpu.VMEM)
        return pl.pallas_call(
            functools.partial(kernel, n_row, n_col, chunks, slots),
            out_shape=jax.ShapeDtypeStruct((rows, width), f32),
            in_specs=[hbm, hbm, hbm, smem, smem],
            out_specs=vmem,
            scratch_shapes=[
                pltpu.VMEM((rows, width), f32),
                pltpu.VMEM((width, width), f32),
                pltpu.VMEM((slots, edge, edge), bf16),
                pltpu.VMEM((chunks, LANES, width), bf16),
                pltpu.VMEM((chunks, LANES, width), bf16),
                pltpu.VMEM((n_row, chunks, rows, LANES), i16),
                pltpu.VMEM((n_row, halves, LANES), f32),
                pltpu.VMEM((n_row, rows, LANES), f32),
                pltpu.VMEM((n_row, rows, 2 * LANES), bf16),
                pltpu.VMEM((n_col + slots + 1, edge, LANES), f32),
                pltpu.VMEM((n_col + slots + 1, edge, LANES), f32),
                pltpu.VMEM((chunks, n_z + 1, rows, LANES), f32),
                pltpu.VMEM((chunks, n_z + 1, rows, LANES), f32),
                pltpu.VMEM((chunks, n_z + 2, rows, LANES), i16),
                pltpu.VMEM((chunks, n_z + 2, halves, LANES), f32),
                pltpu.VMEM((chunks, n_z + 2, rows, LANES), i16),
                pltpu.VMEM((chunks, n_z + 2, halves, LANES), f32),
                pltpu.VMEM((chunks, rows, LANES), f32),
                pltpu.VMEM((chunks, n_z, rows, LANES), f32),
                pltpu.VMEM((n_col, halves, LANES), f32),
                pltpu.VMEM((n_col, halves, LANES), f32),
                pltpu.SMEM((n_col,), jnp.int32),
                pltpu.SMEM((slots,), jnp.int32),
                dma((3,)),
                dma((chunks, n_row)),
                dma((chunks, n_row)),
                dma((n_row,)),
                dma((n_row,)),
                dma((chunks, n_z + 1)),
                dma((chunks, n_z + 1)),
                dma((chunks, n_z + 2)),
                dma((chunks, n_z + 2)),
                dma((chunks, n_z + 2)),
                dma((chunks, n_z + 2)),
                dma((n_col,)),
                dma((n_col,)),
            ],
            compiler_params=pltpu.CompilerParams(
                collective_id=0, has_side_effects=True, vmem_limit_bytes=56 * 1024 * 1024
            ),
        )(
            features,
            weight,
            tile_values.reshape(slots, edge, edge),
            tile_ids.reshape(slots, 2).T,
            tile_counts,
        )

    in_specs = (
        P(("col", "row"), None),
        P(),
        P("row", "col", None, None, None),
        P("row", "col", None, None),
        P("row", "col"),
    )
    out_specs = P(("row", "col"), None)
    return jax.shard_map(shards, mesh=mesh, in_specs=in_specs, out_specs=out_specs, check_vma=False)
```

```python
import functools

import jax
import jax.numpy as jnp
from jax import lax
from jax.experimental import pallas as pl
from jax.experimental.pallas import tpu as pltpu
from jax.sharding import PartitionSpec as P

LANES = 128
CORES = 2
GROUP = 32
AHEAD = 1
QMAX = 32767.0
MESH = pl.DeviceIdType.MESH


def quantize(x, peak):
    inverse = QMAX / peak
    return jnp.round(x * inverse).astype(jnp.int32).astype(jnp.int16)


def row_peak(x):
    return jnp.maximum(jnp.max(jnp.abs(x), axis=1, keepdims=True), 1e-30)


def to_row(column):
    wide = jnp.broadcast_to(column, (LANES, LANES))
    eye = lax.broadcasted_iota(jnp.int32, (LANES, LANES), 0) == lax.broadcasted_iota(
        jnp.int32, (LANES, LANES), 1
    )
    return jnp.sum(jnp.where(eye, wide, 0.0), axis=0, keepdims=True)


def to_columns(row):
    return jnp.broadcast_to(row, (LANES, LANES)).T


def kernel(
    n_row, n_col, chunks, slots,
    feat_hbm, w_hbm, tiles_hbm, ids, count,
    out_ref,
    feat, weight, tiles, w_hi, w_lo,
    gq, gs, gscale, rhs, sums, degs,
    xs, xr, zq, zs, zr, zrs, own, kept, ds, dr,
    last, prevs,
    in_sem, g_send, g_recv, gs_send, gs_recv, x_send, x_recv,
    z_send, z_recv, zs_send, zs_recv, d_send, d_recv,
):
    r = lax.axis_index("row")
    c = lax.axis_index("col")
    n_z = n_col // CORES
    z = c // CORES
    core = c % CORES
    other = 1 - core
    rows = feat.shape[0]
    halves = rows // LANES

    barrier = pltpu.get_barrier_semaphore()

    def greet_row(d, _):
        pl.semaphore_signal(barrier, inc=1, device_id=((r + d) % n_row, c), device_id_type=MESH)
        return 0

    def greet_col(d, _):
        pl.semaphore_signal(barrier, inc=1, device_id=(r, (c + d) % n_col), device_id_type=MESH)
        return 0

    lax.fori_loop(1, n_row, greet_row, 0)
    lax.fori_loop(1, n_col, greet_col, 0)

    load_f = pltpu.make_async_copy(feat_hbm, feat, in_sem.at[0])
    load_t = pltpu.make_async_copy(tiles_hbm, tiles, in_sem.at[1])
    load_w = pltpu.make_async_copy(w_hbm, weight, in_sem.at[2])
    load_f.start()
    load_t.start()
    load_w.start()

    for i in range(n_col):
        last[i] = i

    def link(s, _):
        row = ids[0, s]
        live = s < count[0, 0]
        prevs[s] = last[row]
        for i in range(n_col):
            last[i] = jnp.where(live & (row == i), n_col + s, last[i])
        return 0

    load_f.wait()
    values = feat[...]
    peak = row_peak(values)
    for h in range(halves):
        gs[r, h : h + 1, :] = to_row(peak[h * LANES : (h + 1) * LANES] * (1.0 / QMAX))
    for k in range(chunks):
        gq[r, k] = quantize(values[:, k * LANES : (k + 1) * LANES], peak)

    pl.semaphore_wait(barrier, n_row + n_col - 2)

    def scale_copy(d, source):
        return pltpu.make_async_remote_copy(
            src_ref=gs.at[source], dst_ref=gs.at[source],
            send_sem=gs_send.at[d], recv_sem=gs_recv.at[d],
            device_id=((r + d) % n_row, c), device_id_type=MESH,
        )

    def gather_copy(k, d, source):
        return pltpu.make_async_remote_copy(
            src_ref=gq.at[source, k], dst_ref=gq.at[source, k],
            send_sem=g_send.at[k, d], recv_sem=g_recv.at[k, d],
            device_id=((r + d) % n_row, c), device_id_type=MESH,
        )

    def send_scale(d, _):
        scale_copy(d, r).start()
        return 0

    lax.fori_loop(1, n_row, send_scale, 0)

    def send_gather(k):
        def send(d, _):
            gather_copy(k, d, r).start()
            return 0

        lax.fori_loop(1, n_row, send, 0)

    for k in range(min(AHEAD, chunks)):
        send_gather(k)

    lax.fori_loop(0, slots, link, 0)

    load_t.wait()
    for i in range(n_col):
        sums[i] = jnp.zeros(sums.shape[1:], jnp.float32)

    def degree_copy(d):
        return pltpu.make_async_remote_copy(
            src_ref=ds.at[(c + d) % n_col], dst_ref=dr.at[d],
            send_sem=d_send.at[d], recv_sem=d_recv.at[d],
            device_id=(r, (c + d) % n_col), device_id_type=MESH,
        )

    def core_copy(k, d):
        return pltpu.make_async_remote_copy(
            src_ref=xs.at[k, d], dst_ref=xr.at[k, d],
            send_sem=x_send.at[k, d], recv_sem=x_recv.at[k, d],
            device_id=(r, z * CORES + other), device_id_type=MESH,
        )

    def z_copies(k, d, target):
        return [
            pltpu.make_async_remote_copy(
                src_ref=source.at[k, d], dst_ref=landing.at[k, d],
                send_sem=sent.at[k, d], recv_sem=landed.at[k, d],
                device_id=(r, target * CORES + core), device_id_type=MESH,
            )
            for source, landing, sent, landed in (
                (zs, zrs, zs_send, zs_recv), (zq, zr, z_send, z_recv),
            )
        ]

    top = n_z - 1
    relays = n_z > 2

    def encode(k, d, value):
        peak = row_peak(value)
        for h in range(halves):
            zs[k, d, h : h + 1, :] = to_row(peak[h * LANES : (h + 1) * LANES] * (1.0 / QMAX))
        zq[k, d] = quantize(value, peak)

    def transmit(k, d, target, value):
        encode(k, d, value)
        for copy in z_copies(k, d, target):
            copy.start()

    def distance(t):
        return jnp.where((z == top) | (t == n_z), t, n_z - t)

    def relay(k):
        if not relays:
            return

        @pl.when(z == 1)
        def _():
            transmit(k, top - 1, top, kept[k, top - 1] + received(k, n_z))

        @pl.when(z == top - 1)
        def _():
            transmit(k, 2, 0, kept[k, 2] + received(k, n_z + 1))

    def row_sums():
        for i in range(n_col):
            degs[i] = jnp.zeros(degs.shape[1:], jnp.float32)


        def degree_slot(s, _):
            tile = tiles[s].astype(jnp.float32)
            part = degs[prevs[s]]
            for lane in range(0, tile.shape[1], LANES):
                part = part + tile[:, lane : lane + LANES]
            degs[n_col + s] = part
            return 0

        lax.fori_loop(0, slots, degree_slot, 0, unroll=8)

        def degree_block(i, _):
            total = jnp.sum(degs[last[i]], axis=1, keepdims=True)
            for h in range(halves):
                ds[i, h : h + 1, :] = to_row(total[h * LANES : (h + 1) * LANES])
            return 0

        lax.fori_loop(0, n_col, degree_block, 0, unroll=8)

        def send_degree(d, _):
            degree_copy(d).start()
            return 0

        lax.fori_loop(1, n_col, send_degree, 0)

    def split_weight():
        load_w.wait()
        for k in range(chunks):
            part = weight[k * LANES : (k + 1) * LANES, :]
            high = part.astype(jnp.bfloat16)
            w_hi[k] = high
            w_lo[k] = (part - high.astype(jnp.float32)).astype(jnp.bfloat16)

    def arrive(k, d):
        for copy in z_copies(k, d, jnp.where(z == 0, 1, 0)):
            copy.wait_recv()

    def decoded(k, d):
        parts = []
        for h in range(halves):
            code = zr[k, d, h * LANES : (h + 1) * LANES]
            scale = to_columns(zrs[k, d, h : h + 1, :])
            parts.append(code.astype(jnp.int32).astype(jnp.float32) * scale)
        return jnp.concatenate(parts, axis=0)

    def received(k, d):
        arrive(k, d)
        return decoded(k, d)

    def project(k):
        def is_far(d):
            source = (z + n_z - d) % n_z
            return (((z == 0) & (source == top)) | ((z == top) & (source == 0))) & relays

        def wait_z(d, _):
            @pl.when(jnp.logical_not(is_far(d)))
            def _():
                arrive(k, d)

            return 0

        def add_z(d, total):
            far = is_far(d)
            return total + jnp.where(far, 0.0, decoded(k, jnp.where(far, 2, d)))

        lax.fori_loop(1, n_z, wait_z, 0)
        total = lax.fori_loop(1, n_z, add_z, own[k], unroll=min(n_z - 1, 4))
        high = total.astype(jnp.bfloat16)
        low = (total - high.astype(jnp.float32)).astype(jnp.bfloat16)
        dot = functools.partial(jnp.dot, preferred_element_type=jnp.float32)
        out_ref[...] += dot(high, w_hi[k]) + (dot(high, w_lo[k]) + dot(low, w_hi[k]))

    def one_chunk(k, _):
        def wait_gather(d, _):
            gather_copy(k, d, (r + n_row - d) % n_row).wait_recv()
            return 0

        lax.fori_loop(1, n_row, wait_gather, 0)

        @pl.when(k + AHEAD < chunks)
        def _():
            send_gather(k + AHEAD)

        def decode(j, _):
            value = gq[j, k].astype(jnp.int32).astype(jnp.float32) * gscale[j]
            high = value.astype(jnp.bfloat16)
            rhs[j, :, :LANES] = high
            rhs[j, :, LANES:] = (value - high.astype(jnp.float32)).astype(jnp.bfloat16)
            block = c * n_row + j - r * n_col
            inside = (block >= 0) & (block < n_col)
            sums[jnp.where(inside, block, n_col + slots)] = value
            return 0

        lax.fori_loop(0, n_row, decode, 0, unroll=4)

        def products(g, _):
            for u in range(GROUP):
                s = g * GROUP + u
                both = jnp.dot(tiles[s], rhs[ids[1, s]], preferred_element_type=jnp.float32)
                sums[n_col + s] = both[:, :LANES] + both[:, LANES:] + sums[prevs[s]]
            return 0

        lax.fori_loop(0, slots // GROUP, products, 0)

        def hand_over(t, _):
            d = distance(t)
            zz = (z + d) % n_z
            xs[k, d] = sums[last[zz * CORES + other]]
            core_copy(k, d).start()
            return 0

        lax.fori_loop(1, n_z + 1, hand_over, 0)

        @pl.when(k == 1)
        def _():
            split_weight()

        @pl.when(k >= 1)
        def _():
            relay(k - 1)

        @pl.when(k >= 2)
        def _():
            project(k - 2)

        def route(t):
            d = distance(t)
            zz = (z + d) % n_z
            from_low = (z == 0) & (zz == top) & relays
            from_high = (z == top) & (zz == 0) & relays
            held = (((z == 1) & (zz == top)) | ((z == top - 1) & (zz == 0))) & relays
            slot = jnp.where(from_low, n_z, jnp.where(from_high, n_z + 1, d))
            target = jnp.where(from_low, 1, jnp.where(from_high, top - 1, zz))
            return d, zz, slot, target, held

        def wait_core(t, _):
            core_copy(k, t).wait_recv()
            return 0

        lax.fori_loop(1, n_z + 1, wait_core, 0)

        def code_z(t, _):
            d, zz, slot, target, held = route(t)
            value = sums[last[zz * CORES + core]] + xr[k, d]
            kept[k, d] = value
            encode(k, slot, value)
            return 0

        def send_z(t, _):
            d, zz, slot, target, held = route(t)

            @pl.when(jnp.logical_not(held))
            def _():
                for copy in z_copies(k, slot, target):
                    copy.start()

            return 0

        code_z(1, 0)
        send_z(1, 0)
        lax.fori_loop(2, n_z, code_z, 0, unroll=min(n_z - 2, 4))
        lax.fori_loop(2, n_z, send_z, 0)
        own[k] = sums[last[c]] + xr[k, n_z]
        return 0

    def wait_scale(d, _):
        scale_copy(d, (r + n_row - d) % n_row).wait_recv()
        return 0

    lax.fori_loop(1, n_row, wait_scale, 0)

    def spread_scale(j, _):
        for h in range(halves):
            gscale[j, h * LANES : (h + 1) * LANES, :] = to_columns(gs[j, h : h + 1, :])
        return 0

    lax.fori_loop(0, n_row, spread_scale, 0, unroll=4)
    out_ref[...] = jnp.zeros(out_ref.shape, jnp.float32)
    lax.fori_loop(0, chunks, one_chunk, 0)

    row_sums()
    relay(chunks - 1)
    for k in range(max(chunks - 2, 0), chunks):
        project(k)

    def add_degree(d, total):
        degree_copy(d).wait_recv()
        return total + dr[d]

    degree = lax.fori_loop(1, n_col, add_degree, 1.0 + ds[c])
    root = lax.rsqrt(degree)

    for h in range(halves):
        part = slice(h * LANES, (h + 1) * LANES)
        factor = to_columns(root[h : h + 1, :])
        for k in range(chunks):
            cols = slice(k * LANES, (k + 1) * LANES)
            out_ref[part, cols] = jnp.maximum(out_ref[part, cols] * factor, 0.0)

    def drain_row(d, _):
        scale_copy(d, r).wait_send()

        def drain_chunk(k, _):
            gather_copy(k, d, r).wait_send()
            return 0

        lax.fori_loop(0, chunks, drain_chunk, 0)
        return 0

    def drain_degree(d, _):
        degree_copy(d).wait_send()
        return 0

    def drain_core(k, _):
        def drain_x(d, _):
            core_copy(k, d).wait_send()
            return 0

        lax.fori_loop(1, n_z + 1, drain_x, 0)

        def drain_z(d, _):
            target = (z + d) % n_z
            from_low = (z == 0) & (target == top) & relays
            from_high = (z == top) & (target == 0) & relays
            slot = jnp.where(from_low, n_z, jnp.where(from_high, n_z + 1, d))
            for copy in z_copies(k, slot, target):
                copy.wait_send()
            return 0

        lax.fori_loop(1, n_z, drain_z, 0)
        return 0

    lax.fori_loop(1, n_row, drain_row, 0)
    lax.fori_loop(1, n_col, drain_degree, 0)
    lax.fori_loop(0, chunks, drain_core, 0)


def solution(mesh):
    n_row, n_col = mesh.shape["row"], mesh.shape["col"]
    n_z = n_col // CORES

    def shards(features, weight, tile_values, tile_ids, tile_counts):
        rows, width = features.shape
        slots, edge = tile_values.shape[2], tile_values.shape[3]
        chunks = width // LANES
        halves = rows // LANES
        f32, bf16, i16 = jnp.float32, jnp.bfloat16, jnp.int16
        dma = pltpu.SemaphoreType.DMA
        hbm = pl.BlockSpec(memory_space=pl.ANY)
        smem = pl.BlockSpec(memory_space=pltpu.SMEM)
        vmem = pl.BlockSpec(memory_space=pltpu.VMEM)
        return pl.pallas_call(
            functools.partial(kernel, n_row, n_col, chunks, slots),
            out_shape=jax.ShapeDtypeStruct((rows, width), f32),
            in_specs=[hbm, hbm, hbm, smem, smem],
            out_specs=vmem,
            scratch_shapes=[
                pltpu.VMEM((rows, width), f32),
                pltpu.VMEM((width, width), f32),
                pltpu.VMEM((slots, edge, edge), bf16),
                pltpu.VMEM((chunks, LANES, width), bf16),
                pltpu.VMEM((chunks, LANES, width), bf16),
                pltpu.VMEM((n_row, chunks, rows, LANES), i16),
                pltpu.VMEM((n_row, halves, LANES), f32),
                pltpu.VMEM((n_row, rows, LANES), f32),
                pltpu.VMEM((n_row, rows, 2 * LANES), bf16),
                pltpu.VMEM((n_col + slots + 1, edge, LANES), f32),
                pltpu.VMEM((n_col + slots + 1, edge, LANES), f32),
                pltpu.VMEM((chunks, n_z + 1, rows, LANES), f32),
                pltpu.VMEM((chunks, n_z + 1, rows, LANES), f32),
                pltpu.VMEM((chunks, n_z + 2, rows, LANES), i16),
                pltpu.VMEM((chunks, n_z + 2, halves, LANES), f32),
                pltpu.VMEM((chunks, n_z + 2, rows, LANES), i16),
                pltpu.VMEM((chunks, n_z + 2, halves, LANES), f32),
                pltpu.VMEM((chunks, rows, LANES), f32),
                pltpu.VMEM((chunks, n_z, rows, LANES), f32),
                pltpu.VMEM((n_col, halves, LANES), f32),
                pltpu.VMEM((n_col, halves, LANES), f32),
                pltpu.SMEM((n_col,), jnp.int32),
                pltpu.SMEM((slots,), jnp.int32),
                dma((3,)),
                dma((chunks, n_row)),
                dma((chunks, n_row)),
                dma((n_row,)),
                dma((n_row,)),
                dma((chunks, n_z + 1)),
                dma((chunks, n_z + 1)),
                dma((chunks, n_z + 2)),
                dma((chunks, n_z + 2)),
                dma((chunks, n_z + 2)),
                dma((chunks, n_z + 2)),
                dma((n_col,)),
                dma((n_col,)),
            ],
            compiler_params=pltpu.CompilerParams(
                collective_id=0, has_side_effects=True, vmem_limit_bytes=56 * 1024 * 1024
            ),
        )(
            features,
            weight,
            tile_values.reshape(slots, edge, edge),
            tile_ids.reshape(slots, 2).T,
            tile_counts,
        )

    in_specs = (
        P(("col", "row"), None),
        P(),
        P("row", "col", None, None, None),
        P("row", "col", None, None),
        P("row", "col"),
    )
    out_specs = P(("row", "col"), None)
    return jax.shard_map(shards, mesh=mesh, in_specs=in_specs, out_specs=out_specs, check_vma=False)
```

```python
import functools

import jax
import jax.numpy as jnp
from jax import lax
from jax.experimental import pallas as pl
from jax.experimental.pallas import tpu as pltpu
from jax.sharding import PartitionSpec as P

LANES = 128
CORES = 2
GROUP = 32
AHEAD = 1
QMAX = 32767.0
MESH = pl.DeviceIdType.MESH


def quantize(x, peak):
    inverse = QMAX / peak
    return jnp.round(x * inverse).astype(jnp.int32).astype(jnp.int16)


def row_peak(x):
    return jnp.maximum(jnp.max(jnp.abs(x), axis=1, keepdims=True), 1e-30)


def to_row(column):
    wide = jnp.broadcast_to(column, (LANES, LANES))
    eye = lax.broadcasted_iota(jnp.int32, (LANES, LANES), 0) == lax.broadcasted_iota(
        jnp.int32, (LANES, LANES), 1
    )
    return jnp.sum(jnp.where(eye, wide, 0.0), axis=0, keepdims=True)


def to_columns(row):
    return jnp.broadcast_to(row, (LANES, LANES)).T


def kernel(
    n_row, n_col, chunks, slots,
    feat_hbm, w_hbm, tiles_hbm, ids, count,
    out_ref, root_ref,
    feat, weight, tiles, w_hi, w_lo,
    gq, gs, gscale, rhs, sums, degs,
    xs, xr, zq, zs, zr, zrs, own, kept, ds, dr,
    last, prevs,
    in_sem, g_send, g_recv, gs_send, gs_recv, x_send, x_recv,
    z_send, z_recv, zs_send, zs_recv, d_send, d_recv,
):
    r = lax.axis_index("row")
    c = lax.axis_index("col")
    n_z = n_col // CORES
    z = c // CORES
    core = c % CORES
    other = 1 - core
    rows = feat.shape[0]
    halves = rows // LANES

    barrier = pltpu.get_barrier_semaphore()

    def greet_row(d, _):
        pl.semaphore_signal(barrier, inc=1, device_id=((r + d) % n_row, c), device_id_type=MESH)
        return 0

    def greet_col(d, _):
        pl.semaphore_signal(barrier, inc=1, device_id=(r, (c + d) % n_col), device_id_type=MESH)
        return 0

    lax.fori_loop(1, n_row, greet_row, 0)
    lax.fori_loop(1, n_col, greet_col, 0)

    load_f = pltpu.make_async_copy(feat_hbm, feat, in_sem.at[0])
    load_t = pltpu.make_async_copy(tiles_hbm, tiles, in_sem.at[1])
    load_w = pltpu.make_async_copy(w_hbm, weight, in_sem.at[2])
    load_f.start()
    load_t.start()
    load_w.start()

    for i in range(n_col):
        last[i] = i

    def link(s, _):
        row = ids[0, s]
        live = s < count[0, 0]
        prevs[s] = last[row]
        for i in range(n_col):
            last[i] = jnp.where(live & (row == i), n_col + s, last[i])
        return 0

    load_f.wait()
    values = feat[...]
    peak = row_peak(values)
    for h in range(halves):
        gs[r, h : h + 1, :] = to_row(peak[h * LANES : (h + 1) * LANES] * (1.0 / QMAX))
    for k in range(chunks):
        gq[r, k] = quantize(values[:, k * LANES : (k + 1) * LANES], peak)

    pl.semaphore_wait(barrier, n_row + n_col - 2)

    def scale_copy(d, source):
        return pltpu.make_async_remote_copy(
            src_ref=gs.at[source], dst_ref=gs.at[source],
            send_sem=gs_send.at[d], recv_sem=gs_recv.at[d],
            device_id=((r + d) % n_row, c), device_id_type=MESH,
        )

    def gather_copy(k, d, source):
        return pltpu.make_async_remote_copy(
            src_ref=gq.at[source, k], dst_ref=gq.at[source, k],
            send_sem=g_send.at[k, d], recv_sem=g_recv.at[k, d],
            device_id=((r + d) % n_row, c), device_id_type=MESH,
        )

    def send_scale(d, _):
        scale_copy(d, r).start()
        return 0

    lax.fori_loop(1, n_row, send_scale, 0)

    def send_gather(k):
        def send(d, _):
            gather_copy(k, d, r).start()
            return 0

        lax.fori_loop(1, n_row, send, 0)

    for k in range(min(AHEAD, chunks)):
        send_gather(k)

    lax.fori_loop(0, slots, link, 0)

    load_t.wait()
    for i in range(n_col):
        sums[i] = jnp.zeros(sums.shape[1:], jnp.float32)

    def degree_copy(d):
        return pltpu.make_async_remote_copy(
            src_ref=ds.at[(c + d) % n_col], dst_ref=dr.at[d],
            send_sem=d_send.at[d], recv_sem=d_recv.at[d],
            device_id=(r, (c + d) % n_col), device_id_type=MESH,
        )

    def core_copy(k, d):
        return pltpu.make_async_remote_copy(
            src_ref=xs.at[k, d], dst_ref=xr.at[k, d],
            send_sem=x_send.at[k, d], recv_sem=x_recv.at[k, d],
            device_id=(r, z * CORES + other), device_id_type=MESH,
        )

    def z_copies(k, d, target):
        return [
            pltpu.make_async_remote_copy(
                src_ref=source.at[k, d], dst_ref=landing.at[k, d],
                send_sem=sent.at[k, d], recv_sem=landed.at[k, d],
                device_id=(r, target * CORES + core), device_id_type=MESH,
            )
            for source, landing, sent, landed in (
                (zs, zrs, zs_send, zs_recv), (zq, zr, z_send, z_recv),
            )
        ]

    top = n_z - 1
    relays = n_z > 2

    def encode(k, d, value):
        peak = row_peak(value)
        for h in range(halves):
            zs[k, d, h : h + 1, :] = to_row(peak[h * LANES : (h + 1) * LANES] * (1.0 / QMAX))
        zq[k, d] = quantize(value, peak)

    def transmit(k, d, target, value):
        encode(k, d, value)
        for copy in z_copies(k, d, target):
            copy.start()

    def distance(t):
        return jnp.where((z == top) | (t == n_z), t, n_z - t)

    def relay(k):
        if not relays:
            return

        @pl.when(z == 1)
        def _():
            transmit(k, top - 1, top, kept[k, top - 1] + received(k, n_z))

        @pl.when(z == top - 1)
        def _():
            transmit(k, 2, 0, kept[k, 2] + received(k, n_z + 1))

    def row_sums():
        for i in range(n_col):
            degs[i] = jnp.zeros(degs.shape[1:], jnp.float32)


        def degree_slot(s, _):
            tile = tiles[s].astype(jnp.float32)
            part = degs[prevs[s]]
            for lane in range(0, tile.shape[1], LANES):
                part = part + tile[:, lane : lane + LANES]
            degs[n_col + s] = part
            return 0

        lax.fori_loop(0, slots, degree_slot, 0, unroll=8)

        def degree_block(i, _):
            total = jnp.sum(degs[last[i]], axis=1, keepdims=True)
            for h in range(halves):
                ds[i, h : h + 1, :] = to_row(total[h * LANES : (h + 1) * LANES])
            return 0

        lax.fori_loop(0, n_col, degree_block, 0, unroll=8)

        def send_degree(d, _):
            degree_copy(d).start()
            return 0

        lax.fori_loop(1, n_col, send_degree, 0)

    def split_weight():
        load_w.wait()
        for k in range(chunks):
            part = weight[k * LANES : (k + 1) * LANES, :]
            high = part.astype(jnp.bfloat16)
            w_hi[k] = high
            w_lo[k] = (part - high.astype(jnp.float32)).astype(jnp.bfloat16)

    def arrive(k, d):
        for copy in z_copies(k, d, jnp.where(z == 0, 1, 0)):
            copy.wait_recv()

    def decoded(k, d):
        parts = []
        for h in range(halves):
            code = zr[k, d, h * LANES : (h + 1) * LANES]
            scale = to_columns(zrs[k, d, h : h + 1, :])
            parts.append(code.astype(jnp.int32).astype(jnp.float32) * scale)
        return jnp.concatenate(parts, axis=0)

    def received(k, d):
        arrive(k, d)
        return decoded(k, d)

    def project(k):
        def is_far(d):
            source = (z + n_z - d) % n_z
            return (((z == 0) & (source == top)) | ((z == top) & (source == 0))) & relays

        def wait_z(d, _):
            @pl.when(jnp.logical_not(is_far(d)))
            def _():
                arrive(k, d)

            return 0

        def add_z(d, total):
            far = is_far(d)
            return total + jnp.where(far, 0.0, decoded(k, jnp.where(far, 2, d)))

        lax.fori_loop(1, n_z, wait_z, 0)
        total = lax.fori_loop(1, n_z, add_z, own[k], unroll=min(n_z - 1, 4))
        high = total.astype(jnp.bfloat16)
        low = (total - high.astype(jnp.float32)).astype(jnp.bfloat16)
        dot = functools.partial(jnp.dot, preferred_element_type=jnp.float32)
        out_ref[...] += dot(high, w_hi[k]) + (dot(high, w_lo[k]) + dot(low, w_hi[k]))

    def one_chunk(k, _):
        def wait_gather(d, _):
            gather_copy(k, d, (r + n_row - d) % n_row).wait_recv()
            return 0

        lax.fori_loop(1, n_row, wait_gather, 0)

        @pl.when(k + AHEAD < chunks)
        def _():
            send_gather(k + AHEAD)

        def decode(j, _):
            value = gq[j, k].astype(jnp.int32).astype(jnp.float32) * gscale[j]
            high = value.astype(jnp.bfloat16)
            rhs[j, :, :LANES] = high
            rhs[j, :, LANES:] = (value - high.astype(jnp.float32)).astype(jnp.bfloat16)
            block = c * n_row + j - r * n_col
            inside = (block >= 0) & (block < n_col)
            sums[jnp.where(inside, block, n_col + slots)] = value
            return 0

        lax.fori_loop(0, n_row, decode, 0, unroll=4)

        def products(g, _):
            for u in range(GROUP):
                s = g * GROUP + u
                both = jnp.dot(tiles[s], rhs[ids[1, s]], preferred_element_type=jnp.float32)
                sums[n_col + s] = both[:, :LANES] + both[:, LANES:] + sums[prevs[s]]
            return 0

        lax.fori_loop(0, slots // GROUP, products, 0)

        def hand_over(t, _):
            d = distance(t)
            zz = (z + d) % n_z
            xs[k, d] = sums[last[zz * CORES + other]]
            core_copy(k, d).start()
            return 0

        lax.fori_loop(1, n_z + 1, hand_over, 0)

        @pl.when(k == 1)
        def _():
            split_weight()

        @pl.when(k >= 1)
        def _():
            relay(k - 1)

        @pl.when(k >= 2)
        def _():
            project(k - 2)

        def route(t):
            d = distance(t)
            zz = (z + d) % n_z
            from_low = (z == 0) & (zz == top) & relays
            from_high = (z == top) & (zz == 0) & relays
            held = (((z == 1) & (zz == top)) | ((z == top - 1) & (zz == 0))) & relays
            slot = jnp.where(from_low, n_z, jnp.where(from_high, n_z + 1, d))
            target = jnp.where(from_low, 1, jnp.where(from_high, top - 1, zz))
            return d, zz, slot, target, held

        def code_z(t, _):
            d, zz, slot, target, held = route(t)
            core_copy(k, d).wait_recv()
            value = sums[last[zz * CORES + core]] + xr[k, d]
            kept[k, d] = value
            encode(k, slot, value)

            @pl.when(jnp.logical_not(held))
            def _():
                for copy in z_copies(k, slot, target):
                    copy.start()

            return 0

        lax.fori_loop(1, n_z, code_z, 0)
        core_copy(k, n_z).wait_recv()
        own[k] = sums[last[c]] + xr[k, n_z]
        return 0

    row_sums()

    def wait_scale(d, _):
        scale_copy(d, (r + n_row - d) % n_row).wait_recv()
        return 0

    lax.fori_loop(1, n_row, wait_scale, 0)

    def spread_scale(j, _):
        for h in range(halves):
            gscale[j, h * LANES : (h + 1) * LANES, :] = to_columns(gs[j, h : h + 1, :])
        return 0

    lax.fori_loop(0, n_row, spread_scale, 0, unroll=4)
    out_ref[...] = jnp.zeros(out_ref.shape, jnp.float32)
    lax.fori_loop(0, chunks, one_chunk, 0)

    relay(chunks - 1)
    for k in range(max(chunks - 2, 0), chunks):
        project(k)

    def add_degree(d, total):
        degree_copy(d).wait_recv()
        return total + dr[d]

    degree = lax.fori_loop(1, n_col, add_degree, 1.0 + ds[c])
    root_ref[...] = lax.rsqrt(degree)

    def drain_row(d, _):
        scale_copy(d, r).wait_send()

        def drain_chunk(k, _):
            gather_copy(k, d, r).wait_send()
            return 0

        lax.fori_loop(0, chunks, drain_chunk, 0)
        return 0

    def drain_degree(d, _):
        degree_copy(d).wait_send()
        return 0

    def drain_core(k, _):
        def drain_x(d, _):
            core_copy(k, d).wait_send()
            return 0

        lax.fori_loop(1, n_z + 1, drain_x, 0)

        def drain_z(d, _):
            target = (z + d) % n_z
            from_low = (z == 0) & (target == top) & relays
            from_high = (z == top) & (target == 0) & relays
            slot = jnp.where(from_low, n_z, jnp.where(from_high, n_z + 1, d))
            for copy in z_copies(k, slot, target):
                copy.wait_send()
            return 0

        lax.fori_loop(1, n_z, drain_z, 0)
        return 0

    lax.fori_loop(1, n_row, drain_row, 0)
    lax.fori_loop(1, n_col, drain_degree, 0)
    lax.fori_loop(0, chunks, drain_core, 0)


def finish(sum_ref, root_ref, out_ref):
    for h in range(out_ref.shape[0] // LANES):
        part = slice(h * LANES, (h + 1) * LANES)
        factor = to_columns(root_ref[h : h + 1, :])
        for k in range(out_ref.shape[1] // LANES):
            cols = slice(k * LANES, (k + 1) * LANES)
            out_ref[part, cols] = jnp.maximum(sum_ref[part, cols] * factor, 0.0)


def solution(mesh):
    n_row, n_col = mesh.shape["row"], mesh.shape["col"]
    n_z = n_col // CORES

    def shards(features, weight, tile_values, tile_ids, tile_counts):
        rows, width = features.shape
        slots, edge = tile_values.shape[2], tile_values.shape[3]
        chunks = width // LANES
        halves = rows // LANES
        f32, bf16, i16 = jnp.float32, jnp.bfloat16, jnp.int16
        dma = pltpu.SemaphoreType.DMA
        hbm = pl.BlockSpec(memory_space=pl.ANY)
        smem = pl.BlockSpec(memory_space=pltpu.SMEM)
        vmem = pl.BlockSpec(memory_space=pltpu.VMEM)
        summed, root = pl.pallas_call(
            functools.partial(kernel, n_row, n_col, chunks, slots),
            out_shape=(
                jax.ShapeDtypeStruct((rows, width), f32),
                jax.ShapeDtypeStruct((halves, LANES), f32),
            ),
            in_specs=[hbm, hbm, hbm, smem, smem],
            out_specs=(vmem, vmem),
            scratch_shapes=[
                pltpu.VMEM((rows, width), f32),
                pltpu.VMEM((width, width), f32),
                pltpu.VMEM((slots, edge, edge), bf16),
                pltpu.VMEM((chunks, LANES, width), bf16),
                pltpu.VMEM((chunks, LANES, width), bf16),
                pltpu.VMEM((n_row, chunks, rows, LANES), i16),
                pltpu.VMEM((n_row, halves, LANES), f32),
                pltpu.VMEM((n_row, rows, LANES), f32),
                pltpu.VMEM((n_row, rows, 2 * LANES), bf16),
                pltpu.VMEM((n_col + slots + 1, edge, LANES), f32),
                pltpu.VMEM((n_col + slots + 1, edge, LANES), f32),
                pltpu.VMEM((chunks, n_z + 1, rows, LANES), f32),
                pltpu.VMEM((chunks, n_z + 1, rows, LANES), f32),
                pltpu.VMEM((chunks, n_z + 2, rows, LANES), i16),
                pltpu.VMEM((chunks, n_z + 2, halves, LANES), f32),
                pltpu.VMEM((chunks, n_z + 2, rows, LANES), i16),
                pltpu.VMEM((chunks, n_z + 2, halves, LANES), f32),
                pltpu.VMEM((chunks, rows, LANES), f32),
                pltpu.VMEM((chunks, n_z, rows, LANES), f32),
                pltpu.VMEM((n_col, halves, LANES), f32),
                pltpu.VMEM((n_col, halves, LANES), f32),
                pltpu.SMEM((n_col,), jnp.int32),
                pltpu.SMEM((slots,), jnp.int32),
                dma((3,)),
                dma((chunks, n_row)),
                dma((chunks, n_row)),
                dma((n_row,)),
                dma((n_row,)),
                dma((chunks, n_z + 1)),
                dma((chunks, n_z + 1)),
                dma((chunks, n_z + 2)),
                dma((chunks, n_z + 2)),
                dma((chunks, n_z + 2)),
                dma((chunks, n_z + 2)),
                dma((n_col,)),
                dma((n_col,)),
            ],
            compiler_params=pltpu.CompilerParams(
                collective_id=0, has_side_effects=True, vmem_limit_bytes=56 * 1024 * 1024
            ),
        )(
            features,
            weight,
            tile_values.reshape(slots, edge, edge),
            tile_ids.reshape(slots, 2).T,
            tile_counts,
        )
        return pl.pallas_call(
            finish,
            out_shape=jax.ShapeDtypeStruct((rows, width), f32),
            in_specs=[vmem, vmem],
            out_specs=vmem,
        )(summed, root)

    in_specs = (
        P(("col", "row"), None),
        P(),
        P("row", "col", None, None, None),
        P("row", "col", None, None),
        P("row", "col"),
    )
    out_specs = P(("row", "col"), None)
    return jax.shard_map(shards, mesh=mesh, in_specs=in_specs, out_specs=out_specs, check_vma=False)
```

```python
import functools

import jax
import jax.numpy as jnp
from jax import lax
from jax.experimental import pallas as pl
from jax.experimental.pallas import tpu as pltpu
from jax.sharding import PartitionSpec as P

LANES = 128
CORES = 2
GROUP = 32
AHEAD = 1
QMAX = 32767.0
MESH = pl.DeviceIdType.MESH


def quantize(x, peak):
    inverse = QMAX / peak
    return jnp.round(x * inverse).astype(jnp.int32).astype(jnp.int16)


def row_peak(x):
    return jnp.maximum(jnp.max(jnp.abs(x), axis=1, keepdims=True), 1e-30)


def to_row(column):
    wide = jnp.broadcast_to(column, (LANES, LANES))
    eye = lax.broadcasted_iota(jnp.int32, (LANES, LANES), 0) == lax.broadcasted_iota(
        jnp.int32, (LANES, LANES), 1
    )
    return jnp.sum(jnp.where(eye, wide, 0.0), axis=0, keepdims=True)


def to_columns(row):
    return jnp.broadcast_to(row, (LANES, LANES)).T


def kernel(
    n_row, n_col, chunks, slots,
    feat_hbm, w_hbm, tiles_hbm, ids, count,
    out_ref, root_ref,
    feat, weight, tiles, w_hi, w_lo,
    gq, gs, gscale, rhs, sums, degs,
    xs, xr, zq, zs, zr, zrs, own, kept, ds, dr,
    last, prevs,
    in_sem, g_send, g_recv, gs_send, gs_recv, x_send, x_recv,
    z_send, z_recv, zs_send, zs_recv, d_send, d_recv,
):
    r = lax.axis_index("row")
    c = lax.axis_index("col")
    n_z = n_col // CORES
    z = c // CORES
    core = c % CORES
    other = 1 - core
    rows = feat.shape[0]
    halves = rows // LANES

    barrier = pltpu.get_barrier_semaphore()

    def greet_row(d, _):
        pl.semaphore_signal(barrier, inc=1, device_id=((r + d) % n_row, c), device_id_type=MESH)
        return 0

    def greet_col(d, _):
        pl.semaphore_signal(barrier, inc=1, device_id=(r, (c + d) % n_col), device_id_type=MESH)
        return 0

    lax.fori_loop(1, n_row, greet_row, 0)
    lax.fori_loop(1, n_col, greet_col, 0)

    load_f = pltpu.make_async_copy(feat_hbm, feat, in_sem.at[0])
    load_t = pltpu.make_async_copy(tiles_hbm, tiles, in_sem.at[1])
    load_w = pltpu.make_async_copy(w_hbm, weight, in_sem.at[2])
    load_f.start()
    load_t.start()
    load_w.start()

    for i in range(n_col):
        last[i] = i

    def link(s, _):
        row = ids[0, s]
        live = s < count[0, 0]
        prevs[s] = last[row]
        for i in range(n_col):
            last[i] = jnp.where(live & (row == i), n_col + s, last[i])
        return 0

    load_f.wait()
    values = feat[...]
    peak = row_peak(values)
    for h in range(halves):
        gs[r, h : h + 1, :] = to_row(peak[h * LANES : (h + 1) * LANES] * (1.0 / QMAX))
    for k in range(chunks):
        gq[r, k] = quantize(values[:, k * LANES : (k + 1) * LANES], peak)

    pl.semaphore_wait(barrier, n_row + n_col - 2)

    def scale_copy(d, source):
        return pltpu.make_async_remote_copy(
            src_ref=gs.at[source], dst_ref=gs.at[source],
            send_sem=gs_send.at[d], recv_sem=gs_recv.at[d],
            device_id=((r + d) % n_row, c), device_id_type=MESH,
        )

    def gather_copy(k, d, source):
        return pltpu.make_async_remote_copy(
            src_ref=gq.at[source, k], dst_ref=gq.at[source, k],
            send_sem=g_send.at[k, d], recv_sem=g_recv.at[k, d],
            device_id=((r + d) % n_row, c), device_id_type=MESH,
        )

    def send_scale(d, _):
        scale_copy(d, r).start()
        return 0

    lax.fori_loop(1, n_row, send_scale, 0)

    def send_gather(k):
        def send(d, _):
            gather_copy(k, d, r).start()
            return 0

        lax.fori_loop(1, n_row, send, 0)

    for k in range(min(AHEAD, chunks)):
        send_gather(k)

    lax.fori_loop(0, slots, link, 0)

    load_t.wait()
    for i in range(n_col):
        sums[i] = jnp.zeros(sums.shape[1:], jnp.float32)

    def degree_copy(d):
        return pltpu.make_async_remote_copy(
            src_ref=ds.at[(c + d) % n_col], dst_ref=dr.at[d],
            send_sem=d_send.at[d], recv_sem=d_recv.at[d],
            device_id=(r, (c + d) % n_col), device_id_type=MESH,
        )

    def core_copy(k, d):
        return pltpu.make_async_remote_copy(
            src_ref=xs.at[k, d], dst_ref=xr.at[k, d],
            send_sem=x_send.at[k, d], recv_sem=x_recv.at[k, d],
            device_id=(r, z * CORES + other), device_id_type=MESH,
        )

    def z_copies(k, d, target):
        return [
            pltpu.make_async_remote_copy(
                src_ref=source.at[k, d], dst_ref=landing.at[k, d],
                send_sem=sent.at[k, d], recv_sem=landed.at[k, d],
                device_id=(r, target * CORES + core), device_id_type=MESH,
            )
            for source, landing, sent, landed in (
                (zs, zrs, zs_send, zs_recv), (zq, zr, z_send, z_recv),
            )
        ]

    top = n_z - 1
    relays = n_z > 2

    def encode(k, d, value):
        peak = row_peak(value)
        for h in range(halves):
            zs[k, d, h : h + 1, :] = to_row(peak[h * LANES : (h + 1) * LANES] * (1.0 / QMAX))
        zq[k, d] = quantize(value, peak)

    def transmit(k, d, target, value):
        encode(k, d, value)
        for copy in z_copies(k, d, target):
            copy.start()

    def distance(t):
        return jnp.where((z == top) | (t == n_z), t, n_z - t)

    def relay(k):
        if not relays:
            return

        @pl.when(z == 1)
        def _():
            transmit(k, top - 1, top, kept[k, top - 1] + received(k, n_z))

        @pl.when(z == top - 1)
        def _():
            transmit(k, 2, 0, kept[k, 2] + received(k, n_z + 1))

    def row_sums():
        for i in range(n_col):
            degs[i] = jnp.zeros(degs.shape[1:], jnp.float32)


        def degree_slot(s, _):
            tile = tiles[s].astype(jnp.float32)
            part = degs[prevs[s]]
            for lane in range(0, tile.shape[1], LANES):
                part = part + tile[:, lane : lane + LANES]
            degs[n_col + s] = part
            return 0

        lax.fori_loop(0, slots, degree_slot, 0, unroll=8)

        def degree_block(i, _):
            total = jnp.sum(degs[last[i]], axis=1, keepdims=True)
            for h in range(halves):
                ds[i, h : h + 1, :] = to_row(total[h * LANES : (h + 1) * LANES])
            return 0

        lax.fori_loop(0, n_col, degree_block, 0, unroll=8)

        def send_degree(d, _):
            degree_copy(d).start()
            return 0

        lax.fori_loop(1, n_col, send_degree, 0)

    def split_weight():
        load_w.wait()
        for k in range(chunks):
            part = weight[k * LANES : (k + 1) * LANES, :]
            high = part.astype(jnp.bfloat16)
            w_hi[k] = high
            w_lo[k] = (part - high.astype(jnp.float32)).astype(jnp.bfloat16)

    def arrive(k, d):
        for copy in z_copies(k, d, jnp.where(z == 0, 1, 0)):
            copy.wait_recv()

    def decoded(k, d):
        parts = []
        for h in range(halves):
            code = zr[k, d, h * LANES : (h + 1) * LANES]
            scale = to_columns(zrs[k, d, h : h + 1, :])
            parts.append(code.astype(jnp.int32).astype(jnp.float32) * scale)
        return jnp.concatenate(parts, axis=0)

    def received(k, d):
        arrive(k, d)
        return decoded(k, d)

    def project(k):
        def is_far(d):
            source = (z + n_z - d) % n_z
            return (((z == 0) & (source == top)) | ((z == top) & (source == 0))) & relays

        def wait_z(d, _):
            @pl.when(jnp.logical_not(is_far(d)))
            def _():
                arrive(k, d)

            return 0

        def add_z(d, total):
            far = is_far(d)
            return total + jnp.where(far, 0.0, decoded(k, jnp.where(far, 2, d)))

        lax.fori_loop(1, n_z, wait_z, 0)
        total = lax.fori_loop(1, n_z, add_z, own[k], unroll=min(n_z - 1, 4))
        high = total.astype(jnp.bfloat16)
        low = (total - high.astype(jnp.float32)).astype(jnp.bfloat16)
        dot = functools.partial(jnp.dot, preferred_element_type=jnp.float32)
        out_ref[...] += dot(high, w_hi[k]) + (dot(high, w_lo[k]) + dot(low, w_hi[k]))

    def post(k):
        def route(t):
            d = distance(t)
            zz = (z + d) % n_z
            from_low = (z == 0) & (zz == top) & relays
            from_high = (z == top) & (zz == 0) & relays
            held = (((z == 1) & (zz == top)) | ((z == top - 1) & (zz == 0))) & relays
            slot = jnp.where(from_low, n_z, jnp.where(from_high, n_z + 1, d))
            target = jnp.where(from_low, 1, jnp.where(from_high, top - 1, zz))
            return d, zz, slot, target, held

        def code_z(t, _):
            d, zz, slot, target, held = route(t)
            core_copy(k, d).wait_recv()
            value = kept[k, d] + xr[k, d]
            kept[k, d] = value
            encode(k, slot, value)

            @pl.when(jnp.logical_not(held))
            def _():
                for copy in z_copies(k, slot, target):
                    copy.start()

            return 0

        lax.fori_loop(1, n_z, code_z, 0)
        core_copy(k, n_z).wait_recv()
        own[k] = kept[k, n_z] + xr[k, n_z]

    def one_chunk(k, _):
        def wait_gather(d, _):
            gather_copy(k, d, (r + n_row - d) % n_row).wait_recv()
            return 0

        lax.fori_loop(1, n_row, wait_gather, 0)

        @pl.when(k + AHEAD < chunks)
        def _():
            send_gather(k + AHEAD)

        def decode(j, _):
            value = gq[j, k].astype(jnp.int32).astype(jnp.float32) * gscale[j]
            high = value.astype(jnp.bfloat16)
            rhs[j, :, :LANES] = high
            rhs[j, :, LANES:] = (value - high.astype(jnp.float32)).astype(jnp.bfloat16)
            block = c * n_row + j - r * n_col
            inside = (block >= 0) & (block < n_col)
            sums[jnp.where(inside, block, n_col + slots)] = value
            return 0

        lax.fori_loop(0, n_row, decode, 0, unroll=4)

        def products(g, _):
            for u in range(GROUP):
                s = g * GROUP + u
                both = jnp.dot(tiles[s], rhs[ids[1, s]], preferred_element_type=jnp.float32)
                sums[n_col + s] = both[:, :LANES] + both[:, LANES:] + sums[prevs[s]]
            return 0

        lax.fori_loop(0, slots // GROUP, products, 0)

        def hand_over(t, _):
            d = distance(t)
            zz = (z + d) % n_z
            xs[k, d] = sums[last[zz * CORES + other]]
            core_copy(k, d).start()
            return 0

        lax.fori_loop(1, n_z + 1, hand_over, 0)

        def keep(t, _):
            d = distance(t)
            kept[k, d] = sums[last[(z + d) % n_z * CORES + core]]
            return 0

        lax.fori_loop(1, n_z + 1, keep, 0)

        @pl.when(k == 0)
        def _():
            post(0)

        @pl.when(k == 1)
        def _():
            split_weight()

        @pl.when(k >= 2)
        def _():
            post(k - 1)
            relay(k - 2)

        @pl.when(k >= 3)
        def _():
            project(k - 3)

        return 0

    row_sums()

    def wait_scale(d, _):
        scale_copy(d, (r + n_row - d) % n_row).wait_recv()
        return 0

    lax.fori_loop(1, n_row, wait_scale, 0)

    def spread_scale(j, _):
        for h in range(halves):
            gscale[j, h * LANES : (h + 1) * LANES, :] = to_columns(gs[j, h : h + 1, :])
        return 0

    lax.fori_loop(0, n_row, spread_scale, 0, unroll=4)
    out_ref[...] = jnp.zeros(out_ref.shape, jnp.float32)
    lax.fori_loop(0, chunks, one_chunk, 0)

    if chunks == 1:
        split_weight()
    else:
        post(chunks - 1)
        relay(chunks - 2)
    if chunks >= 3:
        project(chunks - 3)
    relay(chunks - 1)
    for k in range(max(chunks - 2, 0), chunks):
        project(k)

    def add_degree(d, total):
        degree_copy(d).wait_recv()
        return total + dr[d]

    degree = lax.fori_loop(1, n_col, add_degree, 1.0 + ds[c])
    root_ref[...] = lax.rsqrt(degree)

    def drain_row(d, _):
        scale_copy(d, r).wait_send()

        def drain_chunk(k, _):
            gather_copy(k, d, r).wait_send()
            return 0

        lax.fori_loop(0, chunks, drain_chunk, 0)
        return 0

    def drain_degree(d, _):
        degree_copy(d).wait_send()
        return 0

    def drain_core(k, _):
        def drain_x(d, _):
            core_copy(k, d).wait_send()
            return 0

        lax.fori_loop(1, n_z + 1, drain_x, 0)

        def drain_z(d, _):
            target = (z + d) % n_z
            from_low = (z == 0) & (target == top) & relays
            from_high = (z == top) & (target == 0) & relays
            slot = jnp.where(from_low, n_z, jnp.where(from_high, n_z + 1, d))
            for copy in z_copies(k, slot, target):
                copy.wait_send()
            return 0

        lax.fori_loop(1, n_z, drain_z, 0)
        return 0

    lax.fori_loop(1, n_row, drain_row, 0)
    lax.fori_loop(1, n_col, drain_degree, 0)
    lax.fori_loop(0, chunks, drain_core, 0)


def finish(sum_ref, root_ref, out_ref):
    for h in range(out_ref.shape[0] // LANES):
        part = slice(h * LANES, (h + 1) * LANES)
        factor = to_columns(root_ref[h : h + 1, :])
        for k in range(out_ref.shape[1] // LANES):
            cols = slice(k * LANES, (k + 1) * LANES)
            out_ref[part, cols] = jnp.maximum(sum_ref[part, cols] * factor, 0.0)


def solution(mesh):
    n_row, n_col = mesh.shape["row"], mesh.shape["col"]
    n_z = n_col // CORES

    def shards(features, weight, tile_values, tile_ids, tile_counts):
        rows, width = features.shape
        slots, edge = tile_values.shape[2], tile_values.shape[3]
        chunks = width // LANES
        halves = rows // LANES
        f32, bf16, i16 = jnp.float32, jnp.bfloat16, jnp.int16
        dma = pltpu.SemaphoreType.DMA
        hbm = pl.BlockSpec(memory_space=pl.ANY)
        smem = pl.BlockSpec(memory_space=pltpu.SMEM)
        vmem = pl.BlockSpec(memory_space=pltpu.VMEM)
        summed, root = pl.pallas_call(
            functools.partial(kernel, n_row, n_col, chunks, slots),
            out_shape=(
                jax.ShapeDtypeStruct((rows, width), f32),
                jax.ShapeDtypeStruct((halves, LANES), f32),
            ),
            in_specs=[hbm, hbm, hbm, smem, smem],
            out_specs=(vmem, vmem),
            scratch_shapes=[
                pltpu.VMEM((rows, width), f32),
                pltpu.VMEM((width, width), f32),
                pltpu.VMEM((slots, edge, edge), bf16),
                pltpu.VMEM((chunks, LANES, width), bf16),
                pltpu.VMEM((chunks, LANES, width), bf16),
                pltpu.VMEM((n_row, chunks, rows, LANES), i16),
                pltpu.VMEM((n_row, halves, LANES), f32),
                pltpu.VMEM((n_row, rows, LANES), f32),
                pltpu.VMEM((n_row, rows, 2 * LANES), bf16),
                pltpu.VMEM((n_col + slots + 1, edge, LANES), f32),
                pltpu.VMEM((n_col + slots + 1, edge, LANES), f32),
                pltpu.VMEM((chunks, n_z + 1, rows, LANES), f32),
                pltpu.VMEM((chunks, n_z + 1, rows, LANES), f32),
                pltpu.VMEM((chunks, n_z + 2, rows, LANES), i16),
                pltpu.VMEM((chunks, n_z + 2, halves, LANES), f32),
                pltpu.VMEM((chunks, n_z + 2, rows, LANES), i16),
                pltpu.VMEM((chunks, n_z + 2, halves, LANES), f32),
                pltpu.VMEM((chunks, rows, LANES), f32),
                pltpu.VMEM((chunks, n_z + 1, rows, LANES), f32),
                pltpu.VMEM((n_col, halves, LANES), f32),
                pltpu.VMEM((n_col, halves, LANES), f32),
                pltpu.SMEM((n_col,), jnp.int32),
                pltpu.SMEM((slots,), jnp.int32),
                dma((3,)),
                dma((chunks, n_row)),
                dma((chunks, n_row)),
                dma((n_row,)),
                dma((n_row,)),
                dma((chunks, n_z + 1)),
                dma((chunks, n_z + 1)),
                dma((chunks, n_z + 2)),
                dma((chunks, n_z + 2)),
                dma((chunks, n_z + 2)),
                dma((chunks, n_z + 2)),
                dma((n_col,)),
                dma((n_col,)),
            ],
            compiler_params=pltpu.CompilerParams(
                collective_id=0, has_side_effects=True, vmem_limit_bytes=56 * 1024 * 1024
            ),
        )(
            features,
            weight,
            tile_values.reshape(slots, edge, edge),
            tile_ids.reshape(slots, 2).T,
            tile_counts,
        )
        return pl.pallas_call(
            finish,
            out_shape=jax.ShapeDtypeStruct((rows, width), f32),
            in_specs=[vmem, vmem],
            out_specs=vmem,
        )(summed, root)

    in_specs = (
        P(("col", "row"), None),
        P(),
        P("row", "col", None, None, None),
        P("row", "col", None, None),
        P("row", "col"),
    )
    out_specs = P(("row", "col"), None)
    return jax.shard_map(shards, mesh=mesh, in_specs=in_specs, out_specs=out_specs, check_vma=False)
```
